512 devices in a mesh: group: 32 (over y_hi, z), head: 16 (over x, y_lo, core).
Axes of the slice: x: 4, y: 4 (y_hi: 2, y_lo: 2; y = y_hi * 2 + y_lo), z: 16, core: 2. Of those that a mesh axis runs over, the one named last changes fastest.
Arguments:
- queries: bfloat16 [12288, 4096], P(('group', 'head')), may hold values from -130 to 130
- keys: bfloat16 [12288, 4096], P(('group', 'head')), may hold values from -6 to 6
- values: bfloat16 [12288, 4096], P(('group', 'head')), may hold values from -6 to 6
- latent: bfloat16 [12288, 4096], P(('group', 'head')), may hold values from -3 to 3
- levels: int32 [32], replicated, may hold values from 0 to 15
- level_step: float32 [16], replicated, may hold values from 0.5 to 2
- block_mask: int32 [32, 32], replicated, may hold values from 0 to 1, as said below
- leaving: int32 [1], replicated, may hold values from 0 to 31
- entering: bfloat16 [384, 4096], P('head', 'group'), may hold values from -6 to 6
Outputs:
- queue: bfloat16 [12288, 4096], P(('group', 'head'))
The draws below stay inside these ranges and needn't reach their ends.
Inputs may be any that keep to these rules, and one draw needn't show every extreme that they name: block_mask[i, i] = 1 and block_mask[i, j] = 0 for j > i; entries below the diagonal are 0 or 1.
All inputs are finite; a program needn't handle non-finite values.
Results may differ from the reference program's by a relative error of at most 0.0045.
Values may be sent and summed in bfloat16 or wider, within the bound.
A program may use at most 128 MiB of HBM per device.

```python
import math
import jax
import jax.numpy as jnp
from jax import lax

DH = 128
TC = 384
LEVELS = 16
HEADS = 32
HD = 4096
GROUPS = 32
TOKENS = 12288


def shared_keys(key):
    return jnp.clip(jax.random.normal(key, (TOKENS, HD), jnp.float32), -6.0, 6.0)


def draw_keys(key, part):
    common = shared_keys(key)
    return common.astype(jnp.bfloat16)


def draw_queries(key, part):
    key = jax.random.fold_in(key, 2)
    drawn = jnp.clip(1.5 * jax.random.normal(key, (TOKENS, HD), jnp.float32), -9.0, 9.0)
    return drawn.astype(jnp.bfloat16)


def draw_block_mask(key, part):
    key = jax.random.fold_in(key, 3)
    below = (jax.random.randint(key, (GROUPS, GROUPS), 0, 8) != 0).astype(jnp.int32)
    rows = jnp.arange(GROUPS, dtype=jnp.int32)[:, None]
    cols = jnp.arange(GROUPS, dtype=jnp.int32)[None, :]
    return jnp.where(cols < rows, below, 0) + (cols == rows).astype(jnp.int32)


def plant(entries, rng, smallest, high):
    index_at = [jax.random.randint(jax.random.fold_in(rng, axis), (), 0, length) for axis, length in enumerate(entries.shape)]
    widest = entries.shape.index(max(entries.shape))
    neighbour = index_at[:widest] + [(index_at[widest] + 1) % entries.shape[widest]] + index_at[widest + 1:]
    return entries.at[tuple(index_at)].set(smallest).at[tuple(neighbour)].set(high)


def block_scale(stream_key, shape, cuts, smallest, top_value):
    def one(axis_at, parts):
        steps = jax.random.uniform(jax.random.fold_in(jax.random.fold_in(stream_key, 6), axis_at), (parts,), jnp.float32, smallest / len(cuts), top_value / len(cuts))
        return jnp.repeat(jnp.exp(steps), shape[axis_at] // parts).reshape((-1,) + (1,) * (len(shape) - axis_at - 1))

    gain = one(*cuts[0])
    for cut in cuts[1:]:
        gain = gain * one(*cut)
    return gain


def noise(stream_key, shape, scale, limit, split=(), kind=jnp.bfloat16):
    values = scale * jax.random.normal(stream_key, shape, jnp.float32)
    if split:
        values = values * block_scale(stream_key, shape, split, -0.22, 0.18)
    return jnp.clip(values, -limit, limit).astype(kind)


def setup_inputs(seed: int = 0) -> dict:
    arg_keys = jax.random.split(jax.random.key(seed), 10)
    return {
        "queries": draw_queries(jax.random.fold_in(arg_keys[9], 71), 0),
        "keys": draw_keys(jax.random.fold_in(arg_keys[9], 71), 0),
        "values": noise(arg_keys[2], (TOKENS, HD), 1.0, 6.0, ((0, 512),)),
        "latent": noise(arg_keys[3], (TOKENS, HD), 0.5, 3.0, ((0, 512),)),
        "levels": plant(jax.random.randint(arg_keys[4], (GROUPS,), 0, LEVELS), jax.random.fold_in(arg_keys[4], 1), 0, LEVELS - 1).astype(jnp.int32),
        "level_step": jnp.clip(jnp.exp(jax.random.uniform(arg_keys[5], (LEVELS,), jnp.float32, math.log(0.5), math.log(2.0))), 0.5, 2.0),
        "block_mask": draw_block_mask(jax.random.fold_in(arg_keys[9], 71), 0),
        "leaving": jax.random.randint(arg_keys[7], (1,), 0, GROUPS).astype(jnp.int32),
        "entering": noise(arg_keys[8], (TC, HD), 1.0, 6.0, ((0, 16), (1, 32))),
    }


def reference(queries, keys, values, latent, levels, level_step, block_mask, leaving, entering):
    scale = 1.0 / (DH ** 0.5)
    group_of = jnp.arange(TOKENS, dtype=jnp.int32) // TC
    query_blocks = queries.reshape(GROUPS, TC, HEADS, DH)
    key_all = keys.reshape(TOKENS, HEADS, DH).astype(jnp.float32)
    value_all = values.reshape(TOKENS, HEADS, DH).astype(jnp.float32)

    def one_group(pair):
        query, mask_row = pair
        allowed = (mask_row[group_of] > 0)[None, None, :]
        scores = jnp.einsum("rhd,khd->hrk", query.astype(jnp.float32), key_all) * scale
        masked = jnp.where(allowed, scores, -1e30)
        top = jnp.max(masked, axis=2, keepdims=True)
        weights = jnp.where(allowed, jnp.exp(scores - top), 0.0)
        total = jnp.sum(weights, axis=2)
        rounded = weights.astype(jnp.bfloat16).astype(jnp.float32)
        mixed = jnp.einsum("hrk,khd->rhd", rounded, value_all) / jnp.transpose(total)[:, :, None]
        return mixed.astype(jnp.bfloat16).reshape(TC, HD)

    attended = lax.map(one_group, (query_blocks, block_mask)).reshape(TOKENS, HD)
    row_step = level_step[levels][group_of]
    updated = (latent.astype(jnp.float32) + row_step[:, None] * attended.astype(jnp.float32)).astype(jnp.bfloat16)
    spread = jnp.tile(entering, (GROUPS, 1))
    return jnp.where((group_of == leaving[0])[:, None], spread, updated)
```

```python
import functools

import jax
import jax.numpy as jnp
from jax import lax
from jax.experimental import pallas as pl
from jax.experimental.pallas import tpu as pltpu
from jax.sharding import PartitionSpec as P

DH = 128
MESH = pl.DeviceIdType.MESH
LOG2E = 1.4426950408889634
OFF = -1e30
EMPTY = -5e29
LANES = 256
CHUNK = 4
NY = 4


def kernel(
    nz, nx, q_ref, k_ref, v_ref, mask_ref, out_ref,
    swap, stage, qbuf, kvbuf, vt, bias, acc, top, total,
    osend, ssend, orecv, srecv, obuf, abuf, back,
    s0s, s0r, zqs, zqr, zks, zkr, yqs, yqr, xs, xr, os_, or_, ss_, sr_, zos, zor, bs, br,
):
    g = lax.axis_index("group")
    h = lax.axis_index("head")
    yh, z = lax.div(g, nz), lax.rem(g, nz)
    x, yl, core = lax.div(h, 4), lax.rem(lax.div(h, 2), 2), lax.rem(h, 2)
    y = yh * 2 + yl
    rows = q_ref.shape[0]
    slab = 2 * rows
    half = nz * DH
    lanes = nz * slab
    tiles = lanes // LANES
    keys = nx * slab
    chunk_keys = CHUNK * keys
    chunks = nz // CHUNK
    scale = LOG2E / DH**0.5

    def dev(yy, zz, xx, cc):
        return (lax.div(yy, 2) * nz + zz, xx * 4 + lax.rem(yy, 2) * 2 + cc)

    def far(i):
        d = jnp.where(lax.rem(i, 2) == 0, lax.div(i, 2) + 1, nz - lax.div(i + 1, 2))
        return lax.rem(z + d, nz)

    def copy(src, dst, ssem, rsem, where):
        return pltpu.make_async_remote_copy(
            src_ref=src, dst_ref=dst, send_sem=ssem, recv_sem=rsem, device_id=where, device_id_type=MESH
        )

    def loop(lo, hi, f):
        def step(i, carry):
            f(i)
            return carry

        lax.fori_loop(lo, hi, step, 0)

    other = dev(y, z, x, 1 - core)
    xp, xm = lax.rem(x + 1, nx), lax.rem(x + nx - 1, nx)
    ahead, behind = dev(y, z, xp, core), dev(y, z, xm, core)
    ys = [lax.rem(y + d, NY) for d in range(1, NY)]

    barrier = pltpu.get_barrier_semaphore()

    def greet(where):
        pl.semaphore_signal(barrier, inc=1, device_id=where, device_id_type=MESH)

    greet(other)
    greet(ahead)
    greet(behind)
    for yy in ys:
        greet(dev(yy, z, x, core))
    loop(0, nz - 1, lambda i: greet(dev(y, far(i), x, core)))
    pl.semaphore_wait(barrier, 1 + 2 + (NY - 1) + (nz - 1))

    def swap_copy(t):
        ref = (q_ref, k_ref, v_ref)[t]
        cols = pl.ds(pl.multiple_of((1 - core) * half, half), half)
        return copy(ref.at[:, cols], swap.at[t], s0s.at[t], s0r.at[t], other)

    for t in range(3):
        swap_copy(t).start()

    def merge_rows(t):
        ref = (q_ref, k_ref, v_ref)[t]

        def one(zz):
            own = ref[:, pl.ds(pl.multiple_of(core * half + zz * DH, DH), DH)]
            theirs = swap[t, :, pl.ds(pl.multiple_of(zz * DH, DH), DH)]
            both = jnp.concatenate([own.astype(jnp.float32), theirs.astype(jnp.float32)], axis=0)
            stage[t, zz] = both.astype(jnp.bfloat16)

        loop(0, nz, one)

    def at_slab(zz):
        return pl.ds(pl.multiple_of(zz * slab, slab), slab)

    def zq_copy(to, frm):
        return copy(stage.at[0, to], qbuf.at[y, at_slab(frm)], zqs.at[to], zqr.at[frm], dev(y, to, x, core))

    def zk_copy(to, frm):
        return copy(stage.at[pl.ds(1, 2), to], kvbuf.at[:, frm, x], zks.at[to], zkr.at[frm], dev(y, to, x, core))

    swap_copy(0).wait_recv()
    merge_rows(0)
    loop(0, nz - 1, lambda i: zq_copy(far(i), z).start())
    swap_copy(1).wait_recv()
    merge_rows(1)
    swap_copy(2).wait_recv()
    merge_rows(2)
    loop(0, nz - 1, lambda i: zk_copy(far(i), z).start())
    qbuf[y, at_slab(z)] = stage[0, z]
    kvbuf[0, z, x] = stage[1, z]
    kvbuf[1, z, x] = stage[2, z]

    key_rows = mask_ref[pl.ds(pl.multiple_of(yh * nz, nz), nz), :].astype(jnp.float32)
    for b in range(2):
        start = (lax.broadcasted_iota(jnp.int32, (2 * nz, lanes), 0) - b * nz) * slab
        lane = lax.broadcasted_iota(jnp.int32, (2 * nz, lanes), 1)
        pick = jnp.where((lane >= start) & (lane < start + slab), 1.0, 0.0).astype(jnp.float32)
        hit = jnp.dot(key_rows, pick, preferred_element_type=jnp.float32)
        bias[b] = jnp.where(hit > 0.5, 0.0, OFF)

    def clear(i):
        acc[i] = jnp.zeros((DH, LANES), jnp.float32)
        top[i] = jnp.full((8, LANES), EMPTY, jnp.float32)
        total[i] = jnp.zeros((8, LANES), jnp.float32)

    loop(0, NY * tiles, clear)

    def yq_copy(to, frm, d):
        return copy(qbuf.at[frm], qbuf.at[frm], yqs.at[d], yqr.at[frm], dev(to, z, x, core))

    loop(0, nz - 1, lambda i: zq_copy(z, far(i)).wait_recv())
    for d, yy in enumerate(ys):
        @pl.when(lax.div(yy, 2) <= yh)
        def _():
            yq_copy(yy, y, d).start()

    def order(i):
        step = jnp.where(i == 2, 3, jnp.where(i == 3, 2, i))
        return lax.rem(lax.div(z, CHUNK) + step, chunks)

    def part(cc):
        return pl.ds(pl.multiple_of(cc * CHUNK, CHUNK), CHUNK)

    def x_copy(way, cc):
        if way == 0:
            return copy(kvbuf.at[:, part(cc), x], kvbuf.at[:, part(cc), x], xs.at[0, cc], xr.at[0, cc], ahead)
        if way == 1:
            return copy(kvbuf.at[:, part(cc), x], kvbuf.at[:, part(cc), x], xs.at[1, cc], xr.at[1, cc], behind)
        if way == 2:
            return copy(kvbuf.at[0, part(cc), xm], kvbuf.at[0, part(cc), xm], xs.at[2, cc], xr.at[2, cc], ahead)
        return copy(kvbuf.at[1, part(cc), xp], kvbuf.at[1, part(cc), xp], xs.at[3, cc], xr.at[3, cc], behind)

    def bring(i):
        cc = order(i)

        def one(j):
            zz = cc * CHUNK + j

            @pl.when(zz != z)
            def _():
                zk_copy(z, zz).wait_recv()

        loop(0, CHUNK, one)
        x_copy(0, cc).start()
        x_copy(1, cc).start()
        x_copy(0, cc).wait_recv()
        x_copy(2, cc).start()
        x_copy(1, cc).wait_recv()
        x_copy(3, cc).start()

    def attend(i):
        cc = order(i)
        x_copy(2, cc).wait_recv()
        x_copy(3, cc).wait_recv()
        vt[...] = kvbuf[1, part(cc)].reshape(chunk_keys, DH).T

        def tile(n):
            yq, t = lax.div(n, tiles), lax.rem(n, tiles)
            b = lax.div(yq, 2)
            last = lax.div(LANES * t + LANES - 1, slab)

            @pl.when((yh < b) | ((yh == b) & (cc * CHUNK <= last)))
            def _():
                span = pl.ds(pl.multiple_of(t * LANES, LANES), LANES)
                query = qbuf[yq, span]
                key = kvbuf[0, part(cc)].reshape(chunk_keys, DH)
                scores = lax.dot_general(
                    key, query, (((1,), (1,)), ((), ())), preferred_element_type=jnp.float32
                )
                scores = scores * scale
                old = top[n, 0:1]
                new = old
                pieces, shift = [], []
                for j in range(CHUNK):
                    s = scores[j * keys : (j + 1) * keys]
                    off = bias[b, pl.ds(cc * CHUNK + j, 1), span]
                    pieces.append(s)
                    shift.append(off)
                    new = jnp.maximum(new, jnp.max(s, axis=0, keepdims=True) + off)
                carry = jnp.exp2(old - new)
                weights = [jnp.exp2(s + (off - new)) for s, off in zip(pieces, shift)]
                added = sum(jnp.sum(w, axis=0, keepdims=True) for w in weights)
                rounded = jnp.concatenate([w.astype(jnp.bfloat16) for w in weights], axis=0)
                acc[n] = acc[n] * carry + jnp.dot(vt[...], rounded, preferred_element_type=jnp.float32)
                total[n, 0:1] = total[n, 0:1] * carry + added
                top[n, 0:1] = new

        loop(0, NY * tiles, tile)

    bring(0)
    for d, yy in enumerate(ys):
        @pl.when(yh <= lax.div(yy, 2))
        def _():
            yq_copy(y, yy, d).wait_recv()

    def steps(i):
        bring(i)
        attend(i - 1)

    loop(1, chunks, steps)
    attend(chunks - 1)

    def o_copy(to, frm, d):
        return copy(osend.at[d], orecv.at[frm], os_.at[d], or_.at[frm], dev(to, z, x, core))

    def s_copy(to, frm, d):
        return copy(ssend.at[d], srecv.at[frm], ss_.at[d], sr_.at[frm], dev(to, z, x, core))

    for d, yy in enumerate(ys):
        @pl.when(yh <= lax.div(yy, 2))
        def _():
            for t in range(tiles):
                n = yy * tiles + t
                span = pl.ds(t * LANES, LANES)
                sums = total[n, 0:1]
                osend[d, :, span] = (acc[n] / jnp.maximum(sums, 1e-30)).astype(jnp.bfloat16)
                ssend[d, 0:1, span] = top[n, 0:1]
                ssend[d, 1:2, span] = sums
                ssend[d, 2:8, span] = jnp.zeros((6, LANES), jnp.float32)
            s_copy(yy, y, d).start()
            o_copy(yy, y, d).start()

    for d, yy in enumerate(ys):
        @pl.when(lax.div(yy, 2) <= yh)
        def _():
            s_copy(y, yy, d).wait_recv()
            o_copy(y, yy, d).wait_recv()
            for t in range(tiles):
                n = y * tiles + t
                span = pl.ds(t * LANES, LANES)
                theirs = srecv[yy, 0:1, span]
                old = top[n, 0:1]
                new = jnp.maximum(old, theirs)
                keep = jnp.exp2(old - new)
                gain = jnp.exp2(theirs - new) * srecv[yy, 1:2, span]
                acc[n] = acc[n] * keep + orecv[yy, :, span].astype(jnp.float32) * gain
                total[n, 0:1] = total[n, 0:1] * keep + gain
                top[n, 0:1] = new

    for t in range(tiles):
        n = y * tiles + t
        done = acc[n] / total[n, 0:1]
        obuf[pl.ds(t * LANES, LANES)] = done.T.astype(jnp.bfloat16)

    def zo_copy(to, frm):
        return copy(obuf.at[at_slab(to)], abuf.at[frm], zos.at[to], zor.at[frm], dev(y, to, x, core))

    loop(0, nz - 1, lambda i: zo_copy(far(i), z).start())

    def place(zz, block):
        wide = block.astype(jnp.float32)
        col = pl.multiple_of(core * half + zz * DH, DH)
        out_ref[:, pl.ds(col, DH)] = wide[:rows].astype(jnp.bfloat16)
        back[:, pl.ds(pl.multiple_of(zz * DH, DH), DH)] = wide[rows:].astype(jnp.bfloat16)

    place(z, obuf[at_slab(z)])

    def take(i):
        zz = far(i)
        zo_copy(z, zz).wait_recv()
        place(zz, abuf[zz])

    loop(0, nz - 1, take)

    def back_copy(which):
        cols = pl.ds(pl.multiple_of(which * half, half), half)
        return copy(back, out_ref.at[:, cols], bs, br, other)

    back_copy(core).start()

    for t in range(3):
        swap_copy(t).wait_send()

    def sent(i):
        zq_copy(far(i), z).wait_send()
        zk_copy(far(i), z).wait_send()
        zo_copy(far(i), z).wait_send()

    loop(0, nz - 1, sent)
    for d, yy in enumerate(ys):
        @pl.when(lax.div(yy, 2) <= yh)
        def _():
            yq_copy(yy, y, d).wait_send()

        @pl.when(yh <= lax.div(yy, 2))
        def _():
            s_copy(yy, y, d).wait_send()
            o_copy(yy, y, d).wait_send()

    def x_sent(cc):
        for way in range(4):
            x_copy(way, cc).wait_send()

    loop(0, chunks, x_sent)
    back_copy(core).wait_send()
    back_copy(1 - core).wait_recv()


def attended_rows(nz, nx, queries, keys, values, mask_t):
    rows, width = queries.shape
    slab = 2 * rows
    lanes = nz * slab
    tiles = lanes // LANES
    half = nz * DH
    bf, f32 = jnp.bfloat16, jnp.float32
    dma = pltpu.SemaphoreType.DMA
    vmem = pl.BlockSpec(memory_space=pltpu.VMEM)
    scratch = [
        pltpu.VMEM((3, rows, half), bf),
        pltpu.VMEM((3, nz, slab, DH), bf),
        pltpu.VMEM((NY, lanes, DH), bf),
        pltpu.VMEM((2, nz, nx, slab, DH), bf),
        pltpu.VMEM((DH, CHUNK * nx * slab), bf),
        pltpu.VMEM((2, nz, lanes), f32),
        pltpu.VMEM((NY * tiles, DH, LANES), f32),
        pltpu.VMEM((NY * tiles, 8, LANES), f32),
        pltpu.VMEM((NY * tiles, 8, LANES), f32),
        pltpu.VMEM((NY - 1, DH, lanes), bf),
        pltpu.VMEM((NY - 1, 8, lanes), f32),
        pltpu.VMEM((NY, DH, lanes), bf),
        pltpu.VMEM((NY, 8, lanes), f32),
        pltpu.VMEM((lanes, DH), bf),
        pltpu.VMEM((nz, slab, DH), bf),
        pltpu.VMEM((rows, half), bf),
        dma((3,)), dma((3,)),
        dma((nz,)), dma((nz,)), dma((nz,)), dma((nz,)),
        dma((NY - 1,)), dma((NY,)),
        dma((4, nz // CHUNK)), dma((4, nz // CHUNK)),
        dma((NY - 1,)), dma((NY,)), dma((NY - 1,)), dma((NY,)),
        dma((nz,)), dma((nz,)),
        dma, dma,
    ]
    return pl.pallas_call(
        functools.partial(kernel, nz, nx),
        out_shape=jax.ShapeDtypeStruct((rows, width), bf),
        in_specs=[vmem] * 4,
        out_specs=vmem,
        scratch_shapes=scratch,
        compiler_params=pltpu.CompilerParams(
            collective_id=0, has_side_effects=True, vmem_limit_bytes=40 * 2**20
        ),
        cost_estimate=pl.CostEstimate(flops=5 * 10**9, bytes_accessed=10**8, transcendentals=10**7),
        name="attend_planes",
    )(queries, keys, values, mask_t)


def body(queries, keys, values, latent, levels, level_step, block_mask, leaving, entering):
    groups = block_mask.shape[0]
    nz = groups // 2
    nx = lax.axis_size("head") // 4
    mine = lax.axis_index("group")
    gathered = lax.all_gather(entering, "group", axis=0, tiled=True)
    attended = attended_rows(nz, nx, queries, keys, values, block_mask.T)
    level = jnp.sum(jnp.where(jnp.arange(groups, dtype=jnp.int32) == mine, levels, 0))
    step = jnp.sum(
        jnp.where(jnp.arange(level_step.shape[0], dtype=jnp.int32) == level, level_step, 0.0)
    )
    updated = (latent.astype(jnp.float32) + step * attended.astype(jnp.float32)).astype(jnp.bfloat16)
    rows = entering.shape[0]
    entered = gathered.reshape(groups, rows, DH).transpose(1, 0, 2).reshape(rows, groups * DH)
    return jnp.where(mine == leaving[0], entered, updated)


def solution(mesh):
    split = P(("group", "head"), None)
    placed = (split, split, split, split, P(), P(), P(), P(), P("head", "group"))
    return jax.shard_map(body, mesh=mesh, in_specs=placed, out_specs=split, check_vma=False)
```

```python
import functools

import jax
import jax.numpy as jnp
from jax import lax
from jax.experimental import pallas as pl
from jax.experimental.pallas import tpu as pltpu
from jax.sharding import PartitionSpec as P

DH = 128
MESH = pl.DeviceIdType.MESH
LOG2E = 1.4426950408889634
OFF = -1e30
EMPTY = -5e29
CHUNK = 4
NY = 4


def kernel(
    nz, nx, q_ref, k_ref, v_ref, latent_ref, entering_ref, mask_ref, levels_ref, step_ref, leaving_ref, out_ref,
    mine, swap, stage, qbuf, kvbuf, vt, bias, acc, top, total,
    osend, ssend, orecv, srecv, obuf, abuf, back, backr, lat, ebuf,
    ls, s0s, s0r, zqs, zqr, zks, zkr, yqs, yqr, xs, xr, os_, or_, ss_, sr_, zos, zor, es, er, bs, br,
):
    g = lax.axis_index("group")
    h = lax.axis_index("head")
    yh, z = lax.div(g, nz), lax.rem(g, nz)
    x, yl, core = lax.div(h, 4), lax.rem(lax.div(h, 2), 2), lax.rem(h, 2)
    y = yh * 2 + yl
    rows = latent_ref.shape[0]
    slab = 2 * rows
    half = nz * DH
    lanes = nz * slab
    keys = nx * slab
    chunks = nz // CHUNK
    scale = LOG2E / DH**0.5
    inputs = (q_ref, k_ref, v_ref)

    def dev(yy, zz, xx, cc):
        return (lax.div(yy, 2) * nz + zz, xx * 4 + lax.rem(yy, 2) * 2 + cc)

    def turn(o):
        return jnp.where(lax.rem(o, 2) == 1, lax.div(o + 1, 2), nz - lax.div(o, 2))

    def dest(o):
        return lax.rem(z + nz - turn(o), nz)

    def source(o):
        return lax.rem(z + turn(o), nz)

    def copy(src, dst, ssem, rsem, where):
        return pltpu.make_async_remote_copy(
            src_ref=src, dst_ref=dst, send_sem=ssem, recv_sem=rsem, device_id=where, device_id_type=MESH
        )

    def loop(lo, hi, f):
        def step(i, carry):
            f(i)
            return carry

        lax.fori_loop(lo, hi, step, 0)

    other = dev(y, z, x, 1 - core)
    xp, xm = lax.rem(x + 1, nx), lax.rem(x + nx - 1, nx)
    ahead, behind = dev(y, z, xp, core), dev(y, z, xm, core)
    ys = [lax.rem(y + d, NY) for d in range(1, NY)]

    barrier = pltpu.get_barrier_semaphore()

    def greet(where):
        pl.semaphore_signal(barrier, inc=1, device_id=where, device_id_type=MESH)

    loop(1, nz, lambda o: greet(dev(y, dest(o), x, core)))
    for yy in ys:
        greet(dev(yy, z, x, core))
    greet(ahead)
    greet(behind)
    greet(other)

    def columns(which):
        return pl.ds(pl.multiple_of(which * half, half), half)

    local = [pltpu.make_async_copy(inputs[t].at[:, columns(core)], mine.at[t], ls.at[t]) for t in range(3)]
    local.append(pltpu.make_async_copy(latent_ref, lat, ls.at[3]))
    quad, place_in_quad = lax.div(z, 4), lax.rem(z, 4)
    local.append(pltpu.make_async_copy(entering_ref, ebuf.at[yh, quad, place_in_quad], ls.at[4]))
    for c in local:
        c.start()
    pl.semaphore_wait(barrier, 1 + 2 + (NY - 1) + (nz - 1))

    def swap_copy(t):
        return copy(inputs[t].at[:, columns(1 - core)], swap.at[t], s0s.at[t], s0r.at[t], other)

    for t in range(3):
        swap_copy(t).start()

    def merge_rows(t):
        def one(zz):
            cols = pl.ds(pl.multiple_of(zz * DH, DH), DH)
            both = jnp.concatenate([mine[t, :, cols].astype(jnp.float32), swap[t, :, cols].astype(jnp.float32)], axis=0)
            stage[t, zz] = both.astype(jnp.bfloat16)

        loop(0, nz, one)

    def at_slab(zz):
        return pl.ds(pl.multiple_of(zz * slab, slab), slab)

    def zq_copy(o):
        return copy(stage.at[0, dest(o)], qbuf.at[y, at_slab(z)], zqs.at[o], zqr.at[o], dev(y, dest(o), x, core))

    def zk_copy(o):
        return copy(stage.at[pl.ds(1, 2), dest(o)], kvbuf.at[:, o, x], zks.at[o], zkr.at[o], dev(y, dest(o), x, core))

    local[0].wait()
    swap_copy(0).wait_recv()
    merge_rows(0)
    loop(1, nz, lambda o: zq_copy(o).start())
    for t in (1, 2):
        local[t].wait()
        swap_copy(t).wait_recv()
        merge_rows(t)
    loop(1, nz, lambda o: zk_copy(o).start())
    qbuf[y, at_slab(z)] = stage[0, z]
    kvbuf[0, 0, x] = stage[1, z]
    kvbuf[1, 0, x] = stage[2, z]

    def e_copy(n):
        if n < 3:
            block = ebuf.at[yh, quad, place_in_quad]
            where = dev(y, lax.rem(z + 4 * (n + 1), nz), x, core)
        elif n < 6:
            block = ebuf.at[yh, :, place_in_quad]
            where = dev(y, lax.rem(z + (1, 2, nz - 1)[n - 3], nz), x, core)
        else:
            block = ebuf.at[yh]
            where = dev(lax.rem(y + 2, NY), z, x, core)
        return copy(block, block, es.at[n], er.at[n], where)

    local[4].wait()
    for n in range(3):
        e_copy(n).start()

    for b in range(2):
        start = (lax.broadcasted_iota(jnp.int32, (2 * nz, lanes), 0) - b * nz) * slab
        lane = lax.broadcasted_iota(jnp.int32, (2 * nz, lanes), 1)
        pick = jnp.where((lane >= start) & (lane < start + slab), 1.0, 0.0).astype(jnp.float32)
        hit = lax.dot_general(
            mask_ref[...].astype(jnp.float32), pick, (((0,), (0,)), ((), ())), preferred_element_type=jnp.float32
        )
        bias[b] = jnp.where(jnp.where(yh == 0, hit[:nz], hit[nz:]) > 0.5, 0.0, OFF)

    def clear(i):
        acc[i] = jnp.zeros((DH, lanes), jnp.float32)
        top[i] = jnp.full((8, lanes), EMPTY, jnp.float32)
        total[i] = jnp.zeros((8, lanes), jnp.float32)

    loop(0, NY, clear)

    def yq_copy(to, frm):
        return copy(qbuf.at[frm], qbuf.at[frm], yqs.at[to], yqr.at[frm], dev(to, z, x, core))

    loop(1, nz, lambda o: zq_copy(o).wait_recv())
    for yy in ys:
        @pl.when(lax.div(yy, 2) <= yh)
        def _():
            yq_copy(yy, y).start()

    def x_copy(way, i):
        part = pl.ds(i * CHUNK, CHUNK)
        if way < 2:
            block = kvbuf.at[:, part, x]
        else:
            block = kvbuf.at[0, part, xm] if way == 2 else kvbuf.at[1, part, xp]
        return copy(block, block, xs.at[way, i], xr.at[way, i], (ahead, behind)[way % 2])

    def bring(i):
        loop(max(i * CHUNK, 1), (i + 1) * CHUNK, lambda o: zk_copy(o).wait_recv())
        x_copy(0, i).start()
        x_copy(1, i).start()

    def pass_on(i):
        x_copy(0, i).wait_recv()
        x_copy(2, i).start()
        x_copy(1, i).wait_recv()
        x_copy(3, i).start()

    def o_copy(to, frm):
        return copy(osend.at[to], orecv.at[frm], os_.at[to], or_.at[frm], dev(to, z, x, core))

    def s_copy(to, frm):
        return copy(ssend.at[to], srecv.at[frm], ss_.at[to], sr_.at[frm], dev(to, z, x, core))

    def attend(i):
        part = pl.ds(i * CHUNK, CHUNK)
        x_copy(2, i).wait_recv()
        x_copy(3, i).wait_recv()
        vt[...] = kvbuf[1, part].reshape(CHUNK * keys, DH).T

        def softmax(n, b):
            key = kvbuf[0, part].reshape(CHUNK * keys, DH)
            scores = lax.dot_general(
                key, qbuf[n], (((1,), (1,)), ((), ())), preferred_element_type=jnp.float32
            )
            old = top[n, 0:1]
            new = old
            pieces, shift = [], []
            for j in range(CHUNK):
                s = scores[j * keys : (j + 1) * keys]
                off = bias[b, pl.ds(source(i * CHUNK + j), 1), :]
                pieces.append(s)
                shift.append(off)
                new = jnp.maximum(new, jnp.max(s, axis=0, keepdims=True) * scale + off)
            carry = jnp.exp2(old - new)
            weights = [jnp.exp2(s * scale + (off - new)) for s, off in zip(pieces, shift)]
            added = sum(jnp.sum(w, axis=0, keepdims=True) for w in weights)
            total[n, 0:1] = total[n, 0:1] * carry + added
            top[n, 0:1] = new
            return carry, jnp.concatenate([w.astype(jnp.bfloat16) for w in weights], axis=0)

        def side(k):
            b = 1 - k

            @pl.when(yh <= b)
            def _():
                both = [softmax(2 * b + u, b) for u in range(2)]
                for u, (carry, rounded) in enumerate(both):
                    n = 2 * b + u
                    acc[n] = acc[n] * carry + jnp.dot(vt[...], rounded, preferred_element_type=jnp.float32)
                if i == chunks - 1:
                    for u in range(2):
                        send_part(2 * b + u)

        loop(0, 2, side)

    def send_part(n):
        @pl.when(n != y)
        def _():
            sums = total[n, 0:1]
            osend[n] = (acc[n] * (1.0 / jnp.maximum(sums, 1e-30))).astype(jnp.bfloat16)
            ssend[n, 0:1] = top[n, 0:1]
            ssend[n, 1:2] = sums
            ssend[n, 2:8] = jnp.zeros((6, lanes), jnp.float32)
            s_copy(n, y).start()
            o_copy(n, y).start()

    bring(0)
    pass_on(0)
    for yy in ys:
        @pl.when(yh <= lax.div(yy, 2))
        def _():
            yq_copy(y, yy).wait_recv()

    for i in range(chunks):
        if i + 1 < chunks:
            bring(i + 1)
        else:
            for n in range(3):
                e_copy(n).wait_recv()
            for n in range(3, 6):
                e_copy(n).start()
        attend(i)
        if i + 1 < chunks:
            pass_on(i + 1)

    for n in range(3, 6):
        e_copy(n).wait_recv()
    e_copy(6).start()

    for yy in ys:
        @pl.when(lax.div(yy, 2) <= yh)
        def _():
            s_copy(y, yy).wait_recv()
            o_copy(y, yy).wait_recv()
            theirs = srecv[yy, 0:1]
            old = top[y, 0:1]
            new = jnp.maximum(old, theirs)
            keep = jnp.exp2(old - new)
            gain = jnp.exp2(theirs - new) * srecv[yy, 1:2]
            acc[y] = acc[y] * keep + orecv[yy].astype(jnp.float32) * gain
            total[y, 0:1] = total[y, 0:1] * keep + gain
            top[y, 0:1] = new

    obuf[...] = (acc[y] / total[y, 0:1]).T.astype(jnp.bfloat16)

    def zo_copy(o):
        return copy(obuf.at[at_slab(dest(o))], abuf.at[z], zos.at[o], zor.at[o], dev(y, dest(o), x, core))

    def zo_wait(o):
        copy(obuf.at[at_slab(z)], abuf.at[source(o)], zos.at[o], zor.at[o], dev(y, dest(o), x, core)).wait_recv()

    loop(1, nz, lambda o: zo_copy(o).start())

    leaves = leaving_ref[0] == g
    size = step_ref[levels_ref[g]]
    e_copy(6).wait_recv()

    def update(n, rows_of):
        cols = pl.ds(pl.multiple_of(n * DH, DH), DH)
        moved = lat[:, cols].astype(jnp.float32) + size * rows_of
        came = ebuf[lax.div(n, nz), lax.div(lax.rem(n, nz), 4), lax.rem(n, 4)].astype(jnp.float32)
        out_ref[:, cols] = jnp.where(leaves, came, moved).astype(jnp.bfloat16)

    def place(zz, block):
        wide = block.astype(jnp.float32)
        back[:, pl.ds(pl.multiple_of(zz * DH, DH), DH)] = wide[rows:].astype(jnp.bfloat16)
        update(core * nz + zz, wide[:rows])

    local[3].wait()
    place(z, obuf[at_slab(z)])

    def take(o):
        zo_wait(o)
        place(source(o), abuf[source(o)])

    loop(1, nz, take)

    back_copy = copy(back, backr, bs, br, other)
    back_copy.start()

    for t in range(3):
        swap_copy(t).wait_send()

    def sent(o):
        zq_copy(o).wait_send()
        zk_copy(o).wait_send()
        zo_copy(o).wait_send()

    loop(1, nz, sent)
    for yy in ys:
        @pl.when(lax.div(yy, 2) <= yh)
        def _():
            yq_copy(yy, y).wait_send()

        @pl.when(yh <= lax.div(yy, 2))
        def _():
            s_copy(yy, y).wait_send()
            o_copy(yy, y).wait_send()

    for i in range(chunks):
        for way in range(4):
            x_copy(way, i).wait_send()
    for n in range(7):
        e_copy(n).wait_send()
    back_copy.wait()

    def finish(zz):
        cols = pl.ds(pl.multiple_of(zz * DH, DH), DH)
        update((1 - core) * nz + zz, backr[:, cols].astype(jnp.float32))

    loop(0, nz, finish)


def updated_rows(nz, nx, queries, keys, values, latent, entering, block_mask, levels, level_step, leaving):
    rows, width = latent.shape
    slab = 2 * rows
    lanes = nz * slab
    half = nz * DH
    bf, f32 = jnp.bfloat16, jnp.float32
    dma = pltpu.SemaphoreType.DMA
    vmem = pl.BlockSpec(memory_space=pltpu.VMEM)
    smem = pl.BlockSpec(memory_space=pltpu.SMEM)
    anywhere = pl.BlockSpec(memory_space=pl.ANY)
    scratch = [
        pltpu.VMEM((3, rows, half), bf),
        pltpu.VMEM((3, rows, half), bf),
        pltpu.VMEM((3, nz, slab, DH), bf),
        pltpu.VMEM((NY, lanes, DH), bf),
        pltpu.VMEM((2, nz, nx, slab, DH), bf),
        pltpu.VMEM((DH, CHUNK * nx * slab), bf),
        pltpu.VMEM((2, nz, lanes), f32),
        pltpu.VMEM((NY, DH, lanes), f32),
        pltpu.VMEM((NY, 8, lanes), f32),
        pltpu.VMEM((NY, 8, lanes), f32),
        pltpu.VMEM((NY, DH, lanes), bf),
        pltpu.VMEM((NY, 8, lanes), f32),
        pltpu.VMEM((NY, DH, lanes), bf),
        pltpu.VMEM((NY, 8, lanes), f32),
        pltpu.VMEM((lanes, DH), bf),
        pltpu.VMEM((nz, slab, DH), bf),
        pltpu.VMEM((rows, half), bf),
        pltpu.VMEM((rows, half), bf),
        pltpu.VMEM((rows, width), bf),
        pltpu.VMEM((2, nz // 4, 4, rows, DH), bf),
        dma((5,)),
        dma((3,)), dma((3,)),
        dma((nz,)), dma((nz,)), dma((nz,)), dma((nz,)),
        dma((NY,)), dma((NY,)),
        dma((4, nz // CHUNK)), dma((4, nz // CHUNK)),
        dma((NY,)), dma((NY,)), dma((NY,)), dma((NY,)),
        dma((nz,)), dma((nz,)),
        dma((7,)), dma((7,)),
        dma, dma,
    ]
    return pl.pallas_call(
        functools.partial(kernel, nz, nx),
        out_shape=jax.ShapeDtypeStruct((rows, width), bf),
        in_specs=[anywhere] * 5 + [vmem] + [smem] * 3,
        out_specs=vmem,
        scratch_shapes=scratch,
        compiler_params=pltpu.CompilerParams(
            collective_id=0, has_side_effects=True, vmem_limit_bytes=48 * 2**20
        ),
        cost_estimate=pl.CostEstimate(flops=5 * 10**9, bytes_accessed=10**8, transcendentals=10**7),
        name="attend_planes",
    )(queries, keys, values, latent, entering, block_mask, levels, level_step, leaving)


def body(queries, keys, values, latent, levels, level_step, block_mask, leaving, entering):
    nz = block_mask.shape[0] // 2
    nx = lax.axis_size("head") // 4
    return updated_rows(
        nz, nx, queries, keys, values, latent, entering, block_mask, levels, level_step, leaving
    )


def solution(mesh):
    split = P(("group", "head"), None)
    placed = (split, split, split, split, P(), P(), P(), P(), P("head", "group"))
    return jax.shard_map(body, mesh=mesh, in_specs=placed, out_specs=split, check_vma=False)
```

```python
import functools

import jax
import jax.numpy as jnp
from jax import lax
from jax.experimental import pallas as pl
from jax.experimental.pallas import tpu as pltpu
from jax.sharding import PartitionSpec as P

DH = 128
MESH = pl.DeviceIdType.MESH
LOG2E = 1.4426950408889634
OFF = -1e30
EMPTY = -5e29
CHUNK = 4
NY = 4


def kernel(
    nz, nx, q_ref, k_ref, v_ref, latent_ref, entering_ref, mask_ref, levels_ref, step_ref, leaving_ref, out_ref,
    mine, swap, stage, qbuf, kvbuf, vt, bias, acc, top, total,
    osend, ssend, orecv, srecv, obuf, abuf, back, backr, lat, ebuf,
    ls, s0s, s0r, zqs, zqr, zks, zkr, yqs, yqr, xs, xr, os_, or_, ss_, sr_, zos, zor, es, er, bs, br,
):
    g = lax.axis_index("group")
    h = lax.axis_index("head")
    yh, z = lax.div(g, nz), lax.rem(g, nz)
    x, yl, core = lax.div(h, 4), lax.rem(lax.div(h, 2), 2), lax.rem(h, 2)
    y = yh * 2 + yl
    rows = latent_ref.shape[0]
    slab = 2 * rows
    half = nz * DH
    lanes = nz * slab // 2
    near = nz // 2
    keys = nx * slab
    chunks = nz // CHUNK
    scale = LOG2E / DH**0.5
    inputs = (q_ref, k_ref, v_ref)

    def dev(yy, zz, xx, cc):
        return (lax.div(yy, 2) * nz + zz, xx * 4 + lax.rem(yy, 2) * 2 + cc)

    def turn(o):
        return jnp.where(lax.rem(o, 2) == 1, lax.div(o + 1, 2), nz - lax.div(o, 2))

    def dest(o):
        return lax.rem(z + nz - turn(o), nz)

    def source(o):
        return lax.rem(z + turn(o), nz)

    def copy(src, dst, ssem, rsem, where):
        return pltpu.make_async_remote_copy(
            src_ref=src, dst_ref=dst, send_sem=ssem, recv_sem=rsem, device_id=where, device_id_type=MESH
        )

    def loop(lo, hi, f):
        def step(i, carry):
            f(i)
            return carry

        lax.fori_loop(lo, hi, step, 0)

    other = dev(y, z, x, 1 - core)
    xp, xm = lax.rem(x + 1, nx), lax.rem(x + nx - 1, nx)
    ahead, behind = dev(y, z, xp, core), dev(y, z, xm, core)
    ys = [lax.rem(y + d, NY) for d in range(1, NY)]

    barrier = pltpu.get_barrier_semaphore()

    def greet(where):
        pl.semaphore_signal(barrier, inc=1, device_id=where, device_id_type=MESH)

    loop(1, nz, lambda o: greet(dev(y, dest(o), x, core)))
    for yy in ys:
        greet(dev(yy, z, x, core))
    greet(ahead)
    greet(behind)
    greet(other)

    def columns(which):
        return pl.ds(pl.multiple_of(which * half, half), half)

    local = [pltpu.make_async_copy(inputs[t].at[:, columns(core)], mine.at[t], ls.at[t]) for t in range(3)]
    local.append(pltpu.make_async_copy(latent_ref, lat, ls.at[3]))
    quad, place_in_quad = lax.div(z, 4), lax.rem(z, 4)
    local.append(pltpu.make_async_copy(entering_ref, ebuf.at[yh, quad, place_in_quad], ls.at[4]))
    for c in local:
        c.start()
    pl.semaphore_wait(barrier, 1 + 2 + (NY - 1) + (nz - 1))

    def swap_copy(t):
        return copy(inputs[t].at[:, columns(1 - core)], swap.at[t], s0s.at[t], s0r.at[t], other)

    for t in range(3):
        swap_copy(t).start()

    def merge_rows(t):
        def one(zz):
            cols = pl.ds(pl.multiple_of(zz * DH, DH), DH)
            both = jnp.concatenate([mine[t, :, cols].astype(jnp.float32), swap[t, :, cols].astype(jnp.float32)], axis=0)
            stage[t, zz] = both.astype(jnp.bfloat16)

        loop(0, nz, one)

    def at_slab(zz):
        return pl.ds(pl.multiple_of(zz * slab, slab), slab)

    def set_of(o):
        return 1 - lax.div(o, near), at_slab(lax.rem(o, near))

    def zq_copy(o):
        half_set, at = set_of(o)
        return copy(stage.at[0, dest(o)], qbuf.at[half_set, y, at], zqs.at[o], zqr.at[o], dev(y, dest(o), x, core))

    def zk_copy(o):
        return copy(stage.at[pl.ds(1, 2), dest(o)], kvbuf.at[:, o, x], zks.at[o], zkr.at[o], dev(y, dest(o), x, core))

    local[0].wait()
    swap_copy(0).wait_recv()
    merge_rows(0)
    loop(0, near, lambda i: zq_copy(nz - 1 - i).start())
    for t in (1, 2):
        local[t].wait()
        swap_copy(t).wait_recv()
        merge_rows(t)
    loop(1, nz, lambda o: zk_copy(o).start())
    loop(1, near, lambda i: zq_copy(near - i).start())
    qbuf[1, y, at_slab(0)] = stage[0, z]
    kvbuf[0, 0, x] = stage[1, z]
    kvbuf[1, 0, x] = stage[2, z]

    def e_copy(n):
        if n < 3:
            block = ebuf.at[yh, quad, place_in_quad]
            where = dev(y, lax.rem(z + 4 * (n + 1), nz), x, core)
        elif n < 6:
            block = ebuf.at[yh, :, place_in_quad]
            where = dev(y, lax.rem(z + (1, 2, nz - 1)[n - 3], nz), x, core)
        else:
            block = ebuf.at[yh]
            where = dev(lax.rem(y + 2, NY), z, x, core)
        return copy(block, block, es.at[n], er.at[n], where)

    local[4].wait()
    for n in range(3):
        e_copy(n).start()

    lane = lax.broadcasted_iota(jnp.int32, (2 * nz, lanes), 1)
    which = sum(jnp.where(lane >= n * slab, 1, 0) for n in range(1, near))
    row = lax.broadcasted_iota(jnp.int32, (2 * nz, lanes), 0)
    seen = mask_ref[...].astype(jnp.float32)
    for s in range(2):
        o = which + (1 - s) * near
        plane = z + jnp.where((o & 1) == 1, (o + 1) >> 1, nz - (o >> 1))
        plane = jnp.where(plane >= nz, plane - nz, plane)
        for b in range(2):
            pick = jnp.where(row == plane + b * nz, 1.0, 0.0).astype(jnp.float32)
            hit = lax.dot_general(seen, pick, (((0,), (0,)), ((), ())), preferred_element_type=jnp.float32)
            bias[s, b] = jnp.where(jnp.where(yh == 0, hit[:nz], hit[nz:]) > 0.5, 0.0, OFF)

    def clear(i):
        s, n = lax.div(i, NY), lax.rem(i, NY)
        acc[s, n] = jnp.zeros((DH, lanes), jnp.float32)
        top[s, n] = jnp.full((8, lanes), EMPTY, jnp.float32)
        total[s, n] = jnp.zeros((8, lanes), jnp.float32)

    loop(0, 2 * NY, clear)

    def yq_copy(s, to, frm):
        return copy(qbuf.at[s, frm], qbuf.at[s, frm], yqs.at[s, to], yqr.at[s, frm], dev(to, z, x, core))

    def share(s):
        loop(max((1 - s) * near, 1), (2 - s) * near, lambda o: zq_copy(o).wait_recv())
        for yy in ys:
            @pl.when(lax.div(yy, 2) <= yh)
            def _():
                yq_copy(s, yy, y).start()

    def shared(s):
        for yy in ys:
            @pl.when(yh <= lax.div(yy, 2))
            def _():
                yq_copy(s, y, yy).wait_recv()

    def x_copy(way, i):
        part = pl.ds(i * CHUNK, CHUNK)
        if way < 2:
            block = kvbuf.at[:, part, x]
        else:
            block = kvbuf.at[0, part, xm] if way == 2 else kvbuf.at[1, part, xp]
        return copy(block, block, xs.at[way, i], xr.at[way, i], (ahead, behind)[way % 2])

    def bring(i):
        first = i * CHUNK + (1 if isinstance(i, int) and i == 0 else 0)
        loop(first, (i + 1) * CHUNK, lambda o: zk_copy(o).wait_recv())
        x_copy(0, i).start()
        x_copy(1, i).start()

    def pass_on(i):
        x_copy(0, i).wait_recv()
        x_copy(2, i).start()
        x_copy(1, i).wait_recv()
        x_copy(3, i).start()

    def attend(s, i, fresh):
        part = pl.ds(i * CHUNK, CHUNK)
        if fresh:
            x_copy(2, i).wait_recv()
            x_copy(3, i).wait_recv()
            vt[i] = kvbuf[1, part].reshape(CHUNK * keys, DH).T

        def softmax(n):
            key = kvbuf[0, part].reshape(CHUNK * keys, DH)
            scores = lax.dot_general(
                key, qbuf[s, n], (((1,), (1,)), ((), ())), preferred_element_type=jnp.float32
            )
            old = top[s, n, 0:1]
            new = old
            pieces, shift = [], []
            for j in range(CHUNK):
                piece = scores[j * keys : (j + 1) * keys]
                off = bias[s, n // 2, pl.ds(source(i * CHUNK + j), 1), :]
                pieces.append(piece)
                shift.append(off)
                new = jnp.maximum(new, jnp.max(piece, axis=0, keepdims=True) * scale + off)
            carry = jnp.exp2(old - new)
            weights = [jnp.exp2(piece * scale + (off - new)) for piece, off in zip(pieces, shift)]
            added = sum(jnp.sum(w, axis=0, keepdims=True) for w in weights)
            total[s, n, 0:1] = total[s, n, 0:1] * carry + added
            top[s, n, 0:1] = new
            return carry, jnp.concatenate([w.astype(jnp.bfloat16) for w in weights], axis=0)

        def together(sets):
            for n, (carry, rounded) in [(n, softmax(n)) for n in sets]:
                acc[s, n] = acc[s, n] * carry + jnp.dot(vt[i], rounded, preferred_element_type=jnp.float32)

        @pl.when(yh == 0)
        def _():
            together((2, 3, 0, 1))

        @pl.when(yh == 1)
        def _():
            together((2, 3))

    def o_copy(s, to, frm):
        return copy(osend.at[s, to], orecv.at[s, frm], os_.at[s, to], or_.at[s, frm], dev(to, z, x, core))

    def s_copy(s, to, frm):
        return copy(ssend.at[s, to], srecv.at[s, frm], ss_.at[s, to], sr_.at[s, frm], dev(to, z, x, core))

    def send_parts(s):
        for yy in ys:
            @pl.when(yh <= lax.div(yy, 2))
            def _():
                sums = total[s, yy, 0:1]
                osend[s, yy] = (acc[s, yy] * (1.0 / jnp.maximum(sums, 1e-30))).astype(jnp.bfloat16)
                ssend[s, yy, 0:1] = top[s, yy, 0:1]
                ssend[s, yy, 1:2] = sums
                ssend[s, yy, 2:8] = jnp.zeros((6, lanes), jnp.float32)
                s_copy(s, yy, y).start()
                o_copy(s, yy, y).start()

    def merge(s):
        for yy in ys:
            @pl.when(lax.div(yy, 2) <= yh)
            def _():
                s_copy(s, y, yy).wait_recv()
                o_copy(s, y, yy).wait_recv()
                theirs = srecv[s, yy, 0:1]
                old = top[s, y, 0:1]
                new = jnp.maximum(old, theirs)
                keep = jnp.exp2(old - new)
                gain = jnp.exp2(theirs - new) * srecv[s, yy, 1:2]
                acc[s, y] = acc[s, y] * keep + orecv[s, yy].astype(jnp.float32) * gain
                total[s, y, 0:1] = total[s, y, 0:1] * keep + gain
                top[s, y, 0:1] = new
        obuf[s] = (acc[s, y] / total[s, y, 0:1]).T.astype(jnp.bfloat16)

    def zo_copy(o):
        half_set, at = set_of(o)
        to = source(o)
        return copy(obuf.at[half_set, at], abuf.at[o], zos.at[o], zor.at[o], dev(y, to, x, core))

    bring(0)
    pass_on(0)
    share(0)
    shared(0)

    def steps(i):
        bring(i)
        attend(0, i - 1, True)
        pass_on(i)

    loop(1, chunks, steps)
    share(1)
    for n in range(3):
        e_copy(n).wait_recv()
    for n in range(3, 6):
        e_copy(n).start()
    attend(0, chunks - 1, True)
    send_parts(0)
    shared(1)

    def rest(i):
        attend(1, i, False)

        @pl.when(i == 1)
        def _():
            merge(0)
            loop(0, near, lambda j: zo_copy(nz - 1 - j).start())

    loop(0, chunks, rest)
    send_parts(1)
    for n in range(3, 6):
        e_copy(n).wait_recv()
    e_copy(6).start()
    merge(1)
    loop(1, near, lambda j: zo_copy(near - j).start())

    leaves = leaving_ref[0] == g
    size = step_ref[levels_ref[g]]
    local[3].wait()
    e_copy(6).wait_recv()

    def update(n, rows_of):
        cols = pl.ds(pl.multiple_of(n * DH, DH), DH)
        moved = lat[:, cols].astype(jnp.float32) + size * rows_of
        came = ebuf[lax.div(n, nz), lax.div(lax.rem(n, nz), 4), lax.rem(n, 4)].astype(jnp.float32)
        out_ref[:, cols] = jnp.where(leaves, came, moved).astype(jnp.bfloat16)

    def place(o, block):
        wide = block.astype(jnp.float32)
        back[o] = wide[rows:].astype(jnp.bfloat16)
        update(core * nz + dest(o), wide[:rows])

    def take(o):
        zo_copy(o).wait_recv()
        place(o, abuf[o])

    def back_copy(s):
        some = pl.ds((1 - s) * near, near)
        return copy(back.at[some], backr.at[some], bs.at[s], br.at[s], other)

    def finish(s):
        back_copy(s).wait_recv()
        loop((1 - s) * near, (2 - s) * near, lambda o: update((1 - core) * nz + dest(o), backr[o].astype(jnp.float32)))

    loop(0, near, lambda j: take(nz - 1 - j))
    back_copy(0).start()
    place(0, obuf[1, at_slab(0)])
    loop(1, near, lambda j: take(near - j))
    back_copy(1).start()
    finish(0)

    for t in range(3):
        swap_copy(t).wait_send()

    def sent(o):
        zq_copy(o).wait_send()
        zk_copy(o).wait_send()
        zo_copy(o).wait_send()

    loop(1, nz, sent)
    for s in range(2):
        for yy in ys:
            @pl.when(lax.div(yy, 2) <= yh)
            def _():
                yq_copy(s, yy, y).wait_send()

            @pl.when(yh <= lax.div(yy, 2))
            def _():
                s_copy(s, yy, y).wait_send()
                o_copy(s, yy, y).wait_send()

    def x_sent(i):
        for way in range(4):
            x_copy(way, i).wait_send()

    loop(0, chunks, x_sent)
    for n in range(7):
        e_copy(n).wait_send()
    finish(1)
    for s in range(2):
        back_copy(s).wait_send()


def updated_rows(nz, nx, queries, keys, values, latent, entering, block_mask, levels, level_step, leaving):
    rows, width = latent.shape
    slab = 2 * rows
    lanes = nz * slab // 2
    half = nz * DH
    bf, f32 = jnp.bfloat16, jnp.float32
    dma = pltpu.SemaphoreType.DMA
    vmem = pl.BlockSpec(memory_space=pltpu.VMEM)
    smem = pl.BlockSpec(memory_space=pltpu.SMEM)
    hbm = pl.BlockSpec(memory_space=pltpu.HBM)
    scratch = [
        pltpu.VMEM((3, rows, half), bf),
        pltpu.VMEM((3, rows, half), bf),
        pltpu.VMEM((3, nz, slab, DH), bf),
        pltpu.VMEM((2, NY, lanes, DH), bf),
        pltpu.VMEM((2, nz, nx, slab, DH), bf),
        pltpu.VMEM((nz // CHUNK, DH, CHUNK * nx * slab), bf),
        pltpu.VMEM((2, 2, nz, lanes), f32),
        pltpu.VMEM((2, NY, DH, lanes), f32),
        pltpu.VMEM((2, NY, 8, lanes), f32),
        pltpu.VMEM((2, NY, 8, lanes), f32),
        pltpu.VMEM((2, NY, DH, lanes), bf),
        pltpu.VMEM((2, NY, 8, lanes), f32),
        pltpu.VMEM((2, NY, DH, lanes), bf),
        pltpu.VMEM((2, NY, 8, lanes), f32),
        pltpu.VMEM((2, lanes, DH), bf),
        pltpu.VMEM((nz, slab, DH), bf),
        pltpu.VMEM((nz, rows, DH), bf),
        pltpu.VMEM((nz, rows, DH), bf),
        pltpu.VMEM((rows, width), bf),
        pltpu.VMEM((2, nz // 4, 4, rows, DH), bf),
        dma((5,)),
        dma((3,)), dma((3,)),
        dma((nz,)), dma((nz,)), dma((nz,)), dma((nz,)),
        dma((2, NY)), dma((2, NY)),
        dma((4, nz // CHUNK)), dma((4, nz // CHUNK)),
        dma((2, NY)), dma((2, NY)), dma((2, NY)), dma((2, NY)),
        dma((nz,)), dma((nz,)),
        dma((7,)), dma((7,)),
        dma((2,)), dma((2,)),
    ]
    return pl.pallas_call(
        functools.partial(kernel, nz, nx),
        out_shape=jax.ShapeDtypeStruct((rows, width), bf),
        in_specs=[hbm] * 5 + [vmem] + [smem] * 3,
        out_specs=vmem,
        scratch_shapes=scratch,
        compiler_params=pltpu.CompilerParams(
            collective_id=0, has_side_effects=True, vmem_limit_bytes=48 * 2**20
        ),
        cost_estimate=pl.CostEstimate(flops=5 * 10**9, bytes_accessed=10**8, transcendentals=10**7),
        name="attend_planes",
    )(queries, keys, values, latent, entering, block_mask, levels, level_step, leaving)


def body(queries, keys, values, latent, levels, level_step, block_mask, leaving, entering):
    nz = block_mask.shape[0] // 2
    nx = lax.axis_size("head") // 4
    return updated_rows(
        nz, nx, queries, keys, values, latent, entering, block_mask, levels, level_step, leaving
    )


def solution(mesh):
    split = P(("group", "head"), None)
    placed = (split, split, split, split, P(), P(), P(), P(), P("head", "group"))
    return jax.shard_map(body, mesh=mesh, in_specs=placed, out_specs=split, check_vma=False)
```

```python
import functools

import jax
import jax.numpy as jnp
from jax import lax
from jax.experimental import pallas as pl
from jax.experimental.pallas import tpu as pltpu
from jax.sharding import PartitionSpec as P

DH = 128
MESH = pl.DeviceIdType.MESH
LOG2E = 1.4426950408889634
OFF = -1e30
EMPTY = -5e29
CHUNK = 2
FIRST = 3
NY = 4


def kernel(
    nz, nx, q_ref, k_ref, v_ref, latent_ref, entering_ref, mask_ref, levels_ref, step_ref, leaving_ref, out_ref,
    mine, swap, stage, qbuf, kvbuf, vt, bias, acc, top, total,
    osend, ssend, orecv, srecv, obuf, abuf, lat, ebuf,
    ls, s0s, s0r, zqs, zqr, zks, zkr, yqs, yqr, xs, xr, os_, or_, ss_, sr_, zos, zor, es, er,
):
    g = lax.axis_index("group")
    h = lax.axis_index("head")
    yh, z = lax.div(g, nz), lax.rem(g, nz)
    x, yl, core = lax.div(h, 4), lax.rem(lax.div(h, 2), 2), lax.rem(h, 2)
    y = yh * 2 + yl
    rows = latent_ref.shape[0]
    slab = 2 * rows
    half = nz * DH
    lanes = nz * slab // 2
    near = nz // 2
    keys = nx * slab
    chunks = nz // CHUNK
    scale = LOG2E / DH**0.5
    inputs = (q_ref, k_ref, v_ref)

    def dev(yy, zz, xx, cc):
        return (lax.div(yy, 2) * nz + zz, xx * 4 + lax.rem(yy, 2) * 2 + cc)

    def turn(o):
        return jnp.where(lax.rem(o, 2) == 1, lax.div(o + 1, 2), nz - lax.div(o, 2))

    def dest(o):
        return lax.rem(z + nz - turn(o), nz)

    def source(o):
        return lax.rem(z + turn(o), nz)

    def copy(src, dst, ssem, rsem, where):
        return pltpu.make_async_remote_copy(
            src_ref=src, dst_ref=dst, send_sem=ssem, recv_sem=rsem, device_id=where, device_id_type=MESH
        )

    def loop(lo, hi, f):
        def step(i, carry):
            f(i)
            return carry

        lax.fori_loop(lo, hi, step, 0)

    other = dev(y, z, x, 1 - core)
    xs_to = [lax.rem(x + d, nx) for d in (nx // 2, 1, nx - 1)]
    ys = [lax.rem(y + d, NY) for d in range(1, NY)]

    barrier = pltpu.get_barrier_semaphore()

    def greet(where):
        pl.semaphore_signal(barrier, inc=1, device_id=where, device_id_type=MESH)

    def greet_plane(o):
        greet(dev(y, dest(o), x, core))
        greet(dev(y, dest(o), x, 1 - core))

    loop(1, nz, greet_plane)
    for yy in ys:
        greet(dev(yy, z, x, core))
    for to in xs_to:
        greet(dev(y, z, to, core))
    greet(other)

    def columns(which):
        return pl.ds(pl.multiple_of(which * half, half), half)

    local = [pltpu.make_async_copy(inputs[t].at[:, columns(core)], mine.at[t], ls.at[t]) for t in range(3)]
    local.append(pltpu.make_async_copy(latent_ref, lat, ls.at[3]))
    quad, place_in_quad = lax.div(z, 4), lax.rem(z, 4)
    local.append(pltpu.make_async_copy(entering_ref, ebuf.at[yh, quad, place_in_quad], ls.at[4]))
    for c in local:
        c.start()
    pl.semaphore_wait(barrier, 1 + (nx - 1) + (NY - 1) + 2 * (nz - 1))

    def swap_copy(t):
        return copy(inputs[t].at[:, columns(1 - core)], swap.at[t], s0s.at[t], s0r.at[t], other)

    for t in range(3):
        swap_copy(t).start()

    def merge_rows(t):
        def one(zz):
            cols = pl.ds(pl.multiple_of(zz * DH, DH), DH)
            both = jnp.concatenate([mine[t, :, cols].astype(jnp.float32), swap[t, :, cols].astype(jnp.float32)], axis=0)
            stage[t, zz] = both.astype(jnp.bfloat16)

        loop(0, nz, one)

    def at_slab(zz):
        return pl.ds(pl.multiple_of(zz * slab, slab), slab)

    def set_of(o):
        return 1 - lax.div(o, near), at_slab(lax.rem(o, near))

    def zq_copy(o):
        half_set, at = set_of(o)
        return copy(stage.at[0, dest(o)], qbuf.at[half_set, y, at], zqs.at[o], zqr.at[o], dev(y, dest(o), x, core))

    def zk_copy(o):
        return copy(stage.at[pl.ds(1, 2), dest(o)], kvbuf.at[:, o, x], zks.at[o], zkr.at[o], dev(y, dest(o), x, core))

    local[0].wait()
    swap_copy(0).wait_recv()
    merge_rows(0)
    loop(1, nz, lambda i: zq_copy(nz - i).start())
    for t in (1, 2):
        local[t].wait()
        swap_copy(t).wait_recv()
        merge_rows(t)
    loop(1, nz, lambda o: zk_copy(o).start())
    qbuf[1, y, at_slab(0)] = stage[0, z]
    kvbuf[0, 0, x] = stage[1, z]
    kvbuf[1, 0, x] = stage[2, z]

    def e_copy(n):
        if n < 3:
            block = ebuf.at[yh, quad, place_in_quad]
            where = dev(y, lax.rem(z + 4 * (n + 1), nz), x, core)
        elif n < 6:
            block = ebuf.at[yh, :, place_in_quad]
            where = dev(y, lax.rem(z + (1, 2, nz - 1)[n - 3], nz), x, core)
        else:
            block = ebuf.at[yh]
            where = dev(lax.rem(y + 2, NY), z, x, core)
        return copy(block, block, es.at[n], er.at[n], where)


    lane = lax.broadcasted_iota(jnp.int32, (2 * nz, lanes), 1)
    which = sum(jnp.where(lane >= n * slab, 1, 0) for n in range(1, near))
    row = lax.broadcasted_iota(jnp.int32, (2 * nz, lanes), 0)
    seen = mask_ref[...].astype(jnp.float32)
    for s in range(2):
        o = which + (1 - s) * near
        plane = z + jnp.where((o & 1) == 1, (o + 1) >> 1, nz - (o >> 1))
        plane = jnp.where(plane >= nz, plane - nz, plane)
        for b in range(2):
            pick = jnp.where(row == plane + b * nz, 1.0, 0.0).astype(jnp.float32)
            hit = lax.dot_general(seen, pick, (((0,), (0,)), ((), ())), preferred_element_type=jnp.float32)
            bias[s, b] = jnp.where(jnp.where(yh == 0, hit[:nz], hit[nz:]) > 0.5, 0.0, OFF)

    def clear(i):
        s, n = lax.div(i, NY), lax.rem(i, NY)
        acc[s, n] = jnp.zeros((DH, lanes), jnp.float32)
        top[s, n] = jnp.full((8, lanes), EMPTY, jnp.float32)
        total[s, n] = jnp.zeros((8, lanes), jnp.float32)

    loop(0, 2 * NY, clear)

    def yq_copy(s, to, frm):
        return copy(qbuf.at[s, frm], qbuf.at[s, frm], yqs.at[s, to], yqr.at[s, frm], dev(to, z, x, core))

    def share(s):
        loop(max((1 - s) * near, 1), (2 - s) * near, lambda o: zq_copy(o).wait_recv())
        for yy in ys:
            @pl.when(lax.div(yy, 2) <= yh)
            def _():
                yq_copy(s, yy, y).start()

    def shared(s):
        for yy in ys:
            @pl.when(yh <= lax.div(yy, 2))
            def _():
                yq_copy(s, y, yy).wait_recv()

    def x_copy(way, i):
        block = kvbuf.at[:, pl.ds(i * CHUNK, CHUNK), x]
        return copy(block, block, xs.at[way, i], xr.at[way, i], dev(y, z, xs_to[way], core))

    def bring(i):
        first = 1 if isinstance(i, int) and i == 0 else i * CHUNK
        loop(first, (i + 1) * CHUNK, lambda o: zk_copy(o).wait_recv())
        for way in range(nx - 1):
            x_copy(way, i).start()

    def ready(i):
        for way in range(nx - 1):
            x_copy(way, i).wait_recv()
        vt[i] = kvbuf[1, pl.ds(i * CHUNK, CHUNK)].reshape(CHUNK * keys, DH).T

    def attend(s, i, sets):
        part = pl.ds(i * CHUNK, CHUNK)

        def softmax(n):
            key = kvbuf[0, part].reshape(CHUNK * keys, DH)
            scores = lax.dot_general(
                key, qbuf[s, n], (((1,), (1,)), ((), ())), preferred_element_type=jnp.float32
            )
            old = top[s, n, 0:1]
            new = old
            pieces, shift = [], []
            for j in range(CHUNK):
                piece = scores[j * keys : (j + 1) * keys]
                off = bias[s, n // 2, pl.ds(source(i * CHUNK + j), 1), :]
                pieces.append(piece)
                shift.append(off)
                new = jnp.maximum(new, jnp.max(piece, axis=0, keepdims=True) * scale + off)
            carry = jnp.exp2(old - new)
            weights = [jnp.exp2(piece * scale + (off - new)) for piece, off in zip(pieces, shift)]
            added = sum(jnp.sum(w, axis=0, keepdims=True) for w in weights)
            total[s, n, 0:1] = total[s, n, 0:1] * carry + added
            top[s, n, 0:1] = new
            return carry, jnp.concatenate([w.astype(jnp.bfloat16) for w in weights], axis=0)

        for n, (carry, rounded) in [(n, softmax(n)) for n in sets]:
            acc[s, n] = acc[s, n] * carry + jnp.dot(vt[i], rounded, preferred_element_type=jnp.float32)

    def o_copy(s, to, frm):
        return copy(osend.at[s, to], orecv.at[s, frm], os_.at[s, to], or_.at[s, frm], dev(to, z, x, core))

    def s_copy(s, to, frm):
        return copy(ssend.at[s, to], srecv.at[s, frm], ss_.at[s, to], sr_.at[s, frm], dev(to, z, x, core))

    def send_part(s, n):
        @pl.when(n != y)
        def _():
            sums = total[s, n, 0:1]
            osend[s, n] = (acc[s, n] * (1.0 / jnp.maximum(sums, 1e-30))).astype(jnp.bfloat16)
            ssend[s, n, 0:1] = top[s, n, 0:1]
            ssend[s, n, 1:2] = sums
            ssend[s, n, 2:8] = jnp.zeros((6, lanes), jnp.float32)
            s_copy(s, n, y).start()
            o_copy(s, n, y).start()

    def merge(s):
        for yy in ys:
            @pl.when(lax.div(yy, 2) <= yh)
            def _():
                s_copy(s, y, yy).wait_recv()
                o_copy(s, y, yy).wait_recv()
                theirs = srecv[s, yy, 0:1]
                old = top[s, y, 0:1]
                new = jnp.maximum(old, theirs)
                keep = jnp.exp2(old - new)
                gain = jnp.exp2(theirs - new) * srecv[s, yy, 1:2]
                acc[s, y] = acc[s, y] * keep + orecv[s, yy].astype(jnp.float32) * gain
                total[s, y, 0:1] = total[s, y, 0:1] * keep + gain
                top[s, y, 0:1] = new
        done = (acc[s, y] / total[s, y, 0:1]).T
        obuf[s] = done.reshape(near, 2, rows, DH).astype(jnp.bfloat16)

    def zo_copy(o, w):
        block = obuf.at[1 - lax.div(o, near), lax.rem(o, near), w]
        where = dev(y, source(o), x, core if w == 0 else 1 - core)
        return copy(block, abuf.at[w, o], zos.at[w, o], zor.at[w, o], where)

    def give(o):
        zo_copy(o, 0).start()
        zo_copy(o, 1).start()

    share(0)
    bring(0)
    share(1)
    bring(1)
    bring(2)
    shared(0)

    def steps(n):
        early = n < 2 * FIRST
        s = jnp.where(early, lax.div(n, FIRST), lax.rem(n, 2))
        i = jnp.where(early, lax.rem(n, FIRST), lax.div(n, 2))

        @pl.when(n == FIRST)
        def _():
            shared(1)

        @pl.when((s == 0) & ((n == 1) | jnp.logical_not(early)))
        def _():
            bring(jnp.where(early, FIRST, i + 1))

        @pl.when(s == 0)
        def _():
            ready(i)

        @pl.when(yh == 0)
        def _():
            attend(s, i, (2, 3, 0, 1))

        @pl.when(yh == 1)
        def _():
            attend(s, i, (2, 3))

    loop(0, 2 * (chunks - 1), steps)
    local[4].wait()
    for n in range(3):
        e_copy(n).start()

    ready(chunks - 1)

    def last(s):
        attend(s, chunks - 1, (2, 3))
        send_part(s, 2)
        send_part(s, 3)

        @pl.when(yh == 0)
        def _():
            attend(s, chunks - 1, (0, 1))
            send_part(s, 0)
            send_part(s, 1)

    loop(0, 2, last)

    for n in range(3):
        e_copy(n).wait_recv()
    for n in range(3, 6):
        e_copy(n).start()
    merge(0)
    loop(0, near, lambda j: give(nz - 1 - j))
    merge(1)
    loop(1, near, lambda j: give(near - j))
    zo_copy(0, 1).start()
    for n in range(3, 6):
        e_copy(n).wait_recv()
    e_copy(6).start()

    leaves = leaving_ref[0] == g
    size = step_ref[levels_ref[g]]
    local[3].wait()
    e_copy(6).wait_recv()

    def update(n, block):
        cols = pl.ds(pl.multiple_of(n * DH, DH), DH)
        moved = lat[:, cols].astype(jnp.float32) + size * block.astype(jnp.float32)
        came = ebuf[lax.div(n, nz), lax.div(lax.rem(n, nz), 4), lax.rem(n, 4)].astype(jnp.float32)
        out_ref[:, cols] = jnp.where(leaves, came, moved).astype(jnp.bfloat16)

    update(core * nz + z, obuf[1, 0, 0])

    def take(o):
        zo_copy(o, 0).wait_recv()
        update(core * nz + dest(o), abuf[0, o])
        zo_copy(o, 1).wait_recv()
        update((1 - core) * nz + dest(o), abuf[1, o])

    loop(1, nz, lambda j: take(nz - j))
    zo_copy(0, 1).wait_recv()
    update((1 - core) * nz + z, abuf[1, 0])

    for t in range(3):
        swap_copy(t).wait_send()

    def sent(o):
        zq_copy(o).wait_send()
        zk_copy(o).wait_send()
        zo_copy(o, 0).wait_send()
        zo_copy(o, 1).wait_send()

    loop(1, nz, sent)
    zo_copy(0, 1).wait_send()
    for s in range(2):
        for yy in ys:
            @pl.when(lax.div(yy, 2) <= yh)
            def _():
                yq_copy(s, yy, y).wait_send()

            @pl.when(yh <= lax.div(yy, 2))
            def _():
                s_copy(s, yy, y).wait_send()
                o_copy(s, yy, y).wait_send()

    def x_sent(i):
        for way in range(nx - 1):
            x_copy(way, i).wait_send()

    loop(0, chunks, x_sent)
    for n in range(7):
        e_copy(n).wait_send()


def updated_rows(nz, nx, queries, keys, values, latent, entering, block_mask, levels, level_step, leaving):
    rows, width = latent.shape
    slab = 2 * rows
    lanes = nz * slab // 2
    half = nz * DH
    bf, f32 = jnp.bfloat16, jnp.float32
    dma = pltpu.SemaphoreType.DMA
    vmem = pl.BlockSpec(memory_space=pltpu.VMEM)
    smem = pl.BlockSpec(memory_space=pltpu.SMEM)
    hbm = pl.BlockSpec(memory_space=pltpu.HBM)
    scratch = [
        pltpu.VMEM((3, rows, half), bf),
        pltpu.VMEM((3, rows, half), bf),
        pltpu.VMEM((3, nz, slab, DH), bf),
        pltpu.VMEM((2, NY, lanes, DH), bf),
        pltpu.VMEM((2, nz, nx, slab, DH), bf),
        pltpu.VMEM((nz // CHUNK, DH, CHUNK * nx * slab), bf),
        pltpu.VMEM((2, 2, nz, lanes), f32),
        pltpu.VMEM((2, NY, DH, lanes), f32),
        pltpu.VMEM((2, NY, 8, lanes), f32),
        pltpu.VMEM((2, NY, 8, lanes), f32),
        pltpu.VMEM((2, NY, DH, lanes), bf),
        pltpu.VMEM((2, NY, 8, lanes), f32),
        pltpu.VMEM((2, NY, DH, lanes), bf),
        pltpu.VMEM((2, NY, 8, lanes), f32),
        pltpu.VMEM((2, nz // 2, 2, rows, DH), bf),
        pltpu.VMEM((2, nz, rows, DH), bf),
        pltpu.VMEM((rows, width), bf),
        pltpu.VMEM((2, nz // 4, 4, rows, DH), bf),
        dma((5,)),
        dma((3,)), dma((3,)),
        dma((nz,)), dma((nz,)), dma((nz,)), dma((nz,)),
        dma((2, NY)), dma((2, NY)),
        dma((nx - 1, nz // CHUNK)), dma((nx - 1, nz // CHUNK)),
        dma((2, NY)), dma((2, NY)), dma((2, NY)), dma((2, NY)),
        dma((2, nz)), dma((2, nz)),
        dma((7,)), dma((7,)),
    ]
    return pl.pallas_call(
        functools.partial(kernel, nz, nx),
        out_shape=jax.ShapeDtypeStruct((rows, width), bf),
        in_specs=[hbm] * 5 + [vmem] + [smem] * 3,
        out_specs=vmem,
        scratch_shapes=scratch,
        compiler_params=pltpu.CompilerParams(
            collective_id=0, has_side_effects=True, vmem_limit_bytes=63 * 2**20
        ),
        cost_estimate=pl.CostEstimate(flops=5 * 10**9, bytes_accessed=10**8, transcendentals=10**7),
        name="attend_planes",
    )(queries, keys, values, latent, entering, block_mask, levels, level_step, leaving)


def body(queries, keys, values, latent, levels, level_step, block_mask, leaving, entering):
    nz = block_mask.shape[0] // 2
    nx = lax.axis_size("head") // 4
    return updated_rows(
        nz, nx, queries, keys, values, latent, entering, block_mask, levels, level_step, leaving
    )


def solution(mesh):
    split = P(("group", "head"), None)
    placed = (split, split, split, split, P(), P(), P(), P(), P("head", "group"))
    return jax.shard_map(body, mesh=mesh, in_specs=placed, out_specs=split, check_vma=False)
```

```python
import functools

import jax
import jax.numpy as jnp
from jax import lax
from jax.experimental import pallas as pl
from jax.experimental.pallas import tpu as pltpu
from jax.sharding import PartitionSpec as P

DH = 128
MESH = pl.DeviceIdType.MESH
LOG2E = 1.4426950408889634
OFF = -1e30
EMPTY = -5e29
CHUNK = 2
WIDE = 4
PIECES = ((0, 256), (256, 128))
EARLY = 5
NY = 4


def kernel(
    nz, nx, q_ref, k_ref, v_ref, latent_ref, entering_ref, mask_ref, levels_ref, step_ref, leaving_ref, out_ref,
    mine, swap, stage, qbuf, kvbuf, vt, bias, acc, top, total,
    osend, ssend, orecv, srecv, obuf, abuf, lat, ebuf, flat,
    ls, s0s, s0r, zqs, zqr, zks, zkr, yqs, yqr, xs, xr, os_, or_, ss_, sr_, zos, zor, es, er,
):
    g = lax.axis_index("group")
    h = lax.axis_index("head")
    yh, z = lax.div(g, nz), lax.rem(g, nz)
    x, yl, core = lax.div(h, 4), lax.rem(lax.div(h, 2), 2), lax.rem(h, 2)
    y = yh * 2 + yl
    rows = latent_ref.shape[0]
    slab = 2 * rows
    half = nz * DH
    lanes = nz * slab // 2
    near = nz // 2
    keys = nx * slab
    chunks = nz // CHUNK
    scale = LOG2E / DH**0.5
    inputs = (q_ref, k_ref, v_ref)

    def dev(yy, zz, xx, cc):
        return (lax.div(yy, 2) * nz + zz, xx * 4 + lax.rem(yy, 2) * 2 + cc)

    def turn(o):
        return jnp.where(lax.rem(o, 2) == 1, lax.div(o + 1, 2), nz - lax.div(o, 2))

    def dest(o):
        return lax.rem(z + nz - turn(o), nz)

    def source(o):
        return lax.rem(z + turn(o), nz)

    def copy(src, dst, ssem, rsem, where):
        return pltpu.make_async_remote_copy(
            src_ref=src, dst_ref=dst, send_sem=ssem, recv_sem=rsem, device_id=where, device_id_type=MESH
        )

    def loop(lo, hi, f):
        def step(i, carry):
            f(i)
            return carry

        lax.fori_loop(lo, hi, step, 0)

    other = dev(y, z, x, 1 - core)
    xs_to = [lax.rem(x + d, nx) for d in (nx // 2, 1, nx - 1)]
    ys = [lax.rem(y + d, NY) for d in range(1, NY)]

    barrier = pltpu.get_barrier_semaphore()

    def greet(where):
        pl.semaphore_signal(barrier, inc=1, device_id=where, device_id_type=MESH)

    def greet_plane(o):
        greet(dev(y, dest(o), x, core))
        greet(dev(y, dest(o), x, 1 - core))

    loop(1, nz, greet_plane)
    for yy in ys:
        greet(dev(yy, z, x, core))
    for to in xs_to:
        greet(dev(y, z, to, core))
    greet(other)

    def columns(which):
        return pl.ds(pl.multiple_of(which * half, half), half)

    local = [pltpu.make_async_copy(inputs[t].at[:, columns(core)], mine.at[t], ls.at[t]) for t in range(3)]
    local.append(pltpu.make_async_copy(latent_ref, lat, ls.at[3]))
    quad, place_in_quad = lax.div(z, 4), lax.rem(z, 4)
    local.append(pltpu.make_async_copy(entering_ref, ebuf.at[yh, quad, place_in_quad], ls.at[4]))
    for c in local:
        c.start()
    pl.semaphore_wait(barrier, 1 + (nx - 1) + (NY - 1) + 2 * (nz - 1))

    def swap_copy(t):
        return copy(inputs[t].at[:, columns(1 - core)], swap.at[t], s0s.at[t], s0r.at[t], other)

    for t in range(3):
        swap_copy(t).start()

    def merge_rows(t):
        def one(zz):
            cols = pl.ds(pl.multiple_of(zz * DH, DH), DH)
            both = jnp.concatenate([mine[t, :, cols].astype(jnp.float32), swap[t, :, cols].astype(jnp.float32)], axis=0)
            stage[t, zz] = both.astype(jnp.bfloat16)

        loop(0, nz, one)

    def at_slab(zz):
        return pl.ds(pl.multiple_of(zz * slab, slab), slab)

    def place_of(o):
        return jnp.where(o < near, o, nz - 1 - o)

    def set_of(o):
        return 1 - lax.div(o, near), at_slab(place_of(o))

    def zq_copy(o):
        half_set, at = set_of(o)
        return copy(stage.at[0, dest(o)], qbuf.at[half_set, y, at], zqs.at[o], zqr.at[o], dev(y, dest(o), x, core))

    def zk_copy(o):
        return copy(stage.at[pl.ds(1, 2), dest(o)], kvbuf.at[:, o, x], zks.at[o], zkr.at[o], dev(y, dest(o), x, core))

    local[0].wait()
    swap_copy(0).wait_recv()
    merge_rows(0)
    loop(1, nz, lambda i: zq_copy(nz - i).start())
    for t in (1, 2):
        local[t].wait()
        swap_copy(t).wait_recv()
        merge_rows(t)
    loop(1, nz, lambda o: zk_copy(o).start())
    qbuf[1, y, at_slab(0)] = stage[0, z]
    kvbuf[0, 0, x] = stage[1, z]
    kvbuf[1, 0, x] = stage[2, z]

    def e_copy(n):
        if n < 3:
            block = ebuf.at[yh, quad, place_in_quad]
            where = dev(y, lax.rem(z + 4 * (n + 1), nz), x, core)
        elif n < 6:
            block = ebuf.at[yh, :, place_in_quad]
            where = dev(y, lax.rem(z + (1, 2, nz - 1)[n - 3], nz), x, core)
        else:
            block = ebuf.at[yh]
            where = dev(lax.rem(y + 2, NY), z, x, core)
        return copy(block, block, es.at[n], er.at[n], where)


    lane = lax.broadcasted_iota(jnp.int32, (2 * nz, lanes), 1)
    which = sum(jnp.where(lane >= n * slab, 1, 0) for n in range(1, near))
    row = lax.broadcasted_iota(jnp.int32, (2 * nz, lanes), 0)
    seen = mask_ref[...].astype(jnp.float32)
    for s in range(2):
        o = nz - 1 - which if s == 0 else which
        plane = z + jnp.where((o & 1) == 1, (o + 1) >> 1, nz - (o >> 1))
        plane = jnp.where(plane >= nz, plane - nz, plane)
        for b in range(2):
            pick = jnp.where(row == plane + b * nz, 1.0, 0.0).astype(jnp.float32)
            hit = lax.dot_general(seen, pick, (((0,), (0,)), ((), ())), preferred_element_type=jnp.float32)
            bias[s, b] = jnp.where(jnp.where(yh == 0, hit[:nz], hit[nz:]) > 0.5, 0.0, OFF)

    def clear(i):
        s, n = lax.div(i, NY), lax.rem(i, NY)
        acc[s, n] = jnp.zeros((DH, lanes), jnp.float32)
        top[s, n] = jnp.full((8, lanes), EMPTY, jnp.float32)
        total[s, n] = jnp.zeros((8, lanes), jnp.float32)

    loop(0, 2 * NY, clear)

    def yq_copy(s, to, frm):
        return copy(qbuf.at[s, frm], qbuf.at[s, frm], yqs.at[s, to], yqr.at[s, frm], dev(to, z, x, core))

    def share(s):
        loop(max((1 - s) * near, 1), (2 - s) * near, lambda o: zq_copy(o).wait_recv())
        for yy in ys:
            @pl.when(lax.div(yy, 2) <= yh)
            def _():
                yq_copy(s, yy, y).start()

    def shared(s):
        for yy in ys:
            @pl.when(yh <= lax.div(yy, 2))
            def _():
                yq_copy(s, y, yy).wait_recv()

    def x_copy(way, i):
        block = kvbuf.at[:, pl.ds(i * CHUNK, CHUNK), x]
        return copy(block, block, xs.at[way, i], xr.at[way, i], dev(y, z, xs_to[way], core))

    def bring(i):
        first = 1 if isinstance(i, int) and i == 0 else i * CHUNK
        loop(first, (i + 1) * CHUNK, lambda o: zk_copy(o).wait_recv())
        for way in range(nx - 1):
            x_copy(way, i).start()

    def ready(i):
        for way in range(nx - 1):
            x_copy(way, i).wait_recv()
        span = pl.ds(pl.multiple_of(i * CHUNK * keys, CHUNK * keys), CHUNK * keys)
        vt[:, span] = kvbuf[1, pl.ds(i * CHUNK, CHUNK)].reshape(CHUNK * keys, DH).T

    def attend(s, first, planes, sets):
        part = pl.ds(first, planes)
        span = pl.ds(pl.multiple_of(first * keys, CHUNK * keys), planes * keys)

        def softmax(n):
            key = kvbuf[0, part].reshape(planes * keys, DH)
            scores = lax.dot_general(
                key, qbuf[s, n], (((1,), (1,)), ((), ())), preferred_element_type=jnp.float32
            )
            old = top[s, n, 0:1]
            new = old
            pieces, shift = [], []
            for j in range(planes):
                piece = scores[j * keys : (j + 1) * keys]
                off = bias[s, n // 2, pl.ds(source(first + j), 1), :]
                pieces.append(piece)
                shift.append(off)
                new = jnp.maximum(new, jnp.max(piece, axis=0, keepdims=True) * scale + off)
            carry = jnp.exp2(old - new)
            weights = [jnp.exp2(piece * scale + (off - new)) for piece, off in zip(pieces, shift)]
            added = sum(jnp.sum(w, axis=0, keepdims=True) for w in weights)
            total[s, n, 0:1] = total[s, n, 0:1] * carry + added
            top[s, n, 0:1] = new
            return carry, jnp.concatenate([w.astype(jnp.bfloat16) for w in weights], axis=0)

        for n, (carry, rounded) in [(n, softmax(n)) for n in sets]:
            acc[s, n] = acc[s, n] * carry + jnp.dot(vt[:, span], rounded, preferred_element_type=jnp.float32)

    def o_copy(s, p, to, frm):
        part = pl.ds(*PIECES[p])
        return copy(
            osend.at[s, to, :, part], orecv.at[s, frm, :, part], os_.at[p, s, to], or_.at[p, s, frm], dev(to, z, x, core)
        )

    def s_copy(s, to, frm):
        return copy(ssend.at[s, to], srecv.at[s, frm], ss_.at[s, to], sr_.at[s, frm], dev(to, z, x, core))

    def send_part(s, n):
        @pl.when(n != y)
        def _():
            sums = total[s, n, 0:1]
            osend[s, n] = (acc[s, n] * (1.0 / jnp.maximum(sums, 1e-30))).astype(jnp.bfloat16)
            ssend[s, n, 0:1] = top[s, n, 0:1]
            ssend[s, n, 1:2] = sums
            s_copy(s, n, y).start()
            for p in range(len(PIECES)):
                o_copy(s, p, n, y).start()

    def merge(s, p):
        part = pl.ds(*PIECES[p])
        for yy in ys:
            @pl.when(lax.div(yy, 2) <= yh)
            def _():
                if p == 0:
                    s_copy(s, y, yy).wait_recv()
                o_copy(s, p, y, yy).wait_recv()
                theirs = srecv[s, yy, 0:1, part]
                old = top[s, y, 0:1, part]
                new = jnp.maximum(old, theirs)
                keep = jnp.exp2(old - new)
                gain = jnp.exp2(theirs - new) * srecv[s, yy, 1:2, part]
                acc[s, y, :, part] = acc[s, y, :, part] * keep + orecv[s, yy, :, part].astype(jnp.float32) * gain
                total[s, y, 0:1, part] = total[s, y, 0:1, part] * keep + gain
                top[s, y, 0:1, part] = new
        flat[part] = (acc[s, y, :, part] / total[s, y, 0:1, part]).T
        first, until = (0, EARLY) if p == 0 else (EARLY, near)
        some = flat[first * slab : until * slab].reshape(until - first, 2, rows, DH)
        obuf[s, first:until] = some.astype(jnp.bfloat16)

    def zo_copy(o, w):
        block = obuf.at[1 - lax.div(o, near), place_of(o), w]
        where = dev(y, source(o), x, core if w == 0 else 1 - core)
        return copy(block, abuf.at[w, o], zos.at[w, o], zor.at[w, o], where)

    def give(o):
        zo_copy(o, 0).start()
        zo_copy(o, 1).start()

    share(0)
    bring(0)
    share(1)
    bring(1)
    shared(0)

    def steps(n):
        s, w = lax.rem(n, 2), lax.div(n, 2)

        @pl.when(s == 0)
        def _():
            bring(2 * w + 2)
            ready(2 * w)
            ready(2 * w + 1)

        @pl.when(n == 1)
        def _():
            shared(1)

        @pl.when(s == 1)
        def _():
            bring(2 * w + 3)

        @pl.when(yh == 0)
        def _():
            attend(s, w * WIDE, WIDE, (2, 3, 0, 1))

        @pl.when(yh == 1)
        def _():
            attend(s, w * WIDE, WIDE, (2, 3))

    loop(0, 2 * (nz // WIDE - 1), steps)
    local[4].wait()
    for n in range(3):
        e_copy(n).start()

    def upper(n):
        s, i = lax.rem(n, 2), chunks - 2 + lax.div(n, 2)

        @pl.when(s == 0)
        def _():
            ready(i)

        attend(s, i * CHUNK, CHUNK, (2, 3))

        @pl.when(i == chunks - 1)
        def _():
            send_part(s, 2)
            send_part(s, 3)

    loop(0, 4, upper)

    def lower(s):
        attend(s, nz - WIDE, WIDE, (0, 1))
        send_part(s, 0)
        send_part(s, 1)

    @pl.when(yh == 0)
    def _():
        loop(0, 2, lower)

    for n in range(3):
        e_copy(n).wait_recv()
    for n in range(3, 6):
        e_copy(n).start()
    merge(0, 0)
    loop(0, EARLY, lambda j: give(nz - 1 - j))
    merge(0, 1)
    loop(EARLY, near, lambda j: give(nz - 1 - j))
    merge(1, 0)
    merge(1, 1)
    loop(1, near, lambda j: give(near - j))
    zo_copy(0, 1).start()
    for n in range(3, 6):
        e_copy(n).wait_recv()
    e_copy(6).start()

    leaves = leaving_ref[0] == g
    size = step_ref[levels_ref[g]]
    local[3].wait()
    e_copy(6).wait_recv()

    def update(n, block):
        cols = pl.ds(pl.multiple_of(n * DH, DH), DH)
        moved = lat[:, cols].astype(jnp.float32) + size * block.astype(jnp.float32)
        came = ebuf[lax.div(n, nz), lax.div(lax.rem(n, nz), 4), lax.rem(n, 4)].astype(jnp.float32)
        out_ref[:, cols] = jnp.where(leaves, came, moved).astype(jnp.bfloat16)

    update(core * nz + z, obuf[1, 0, 0])

    def take(o):
        zo_copy(o, 0).wait_recv()
        update(core * nz + dest(o), abuf[0, o])
        zo_copy(o, 1).wait_recv()
        update((1 - core) * nz + dest(o), abuf[1, o])

    loop(1, nz, lambda j: take(nz - j))
    zo_copy(0, 1).wait_recv()
    update((1 - core) * nz + z, abuf[1, 0])

    for t in range(3):
        swap_copy(t).wait_send()

    def sent(o):
        zq_copy(o).wait_send()
        zk_copy(o).wait_send()
        zo_copy(o, 0).wait_send()
        zo_copy(o, 1).wait_send()

    loop(1, nz, sent)
    zo_copy(0, 1).wait_send()
    for s in range(2):
        for yy in ys:
            @pl.when(lax.div(yy, 2) <= yh)
            def _():
                yq_copy(s, yy, y).wait_send()

            @pl.when(yh <= lax.div(yy, 2))
            def _():
                s_copy(s, yy, y).wait_send()
                for p in range(len(PIECES)):
                    o_copy(s, p, yy, y).wait_send()

    def x_sent(i):
        for way in range(nx - 1):
            x_copy(way, i).wait_send()

    loop(0, chunks, x_sent)
    for n in range(7):
        e_copy(n).wait_send()


def updated_rows(nz, nx, queries, keys, values, latent, entering, block_mask, levels, level_step, leaving):
    rows, width = latent.shape
    slab = 2 * rows
    lanes = nz * slab // 2
    half = nz * DH
    bf, f32 = jnp.bfloat16, jnp.float32
    dma = pltpu.SemaphoreType.DMA
    vmem = pl.BlockSpec(memory_space=pltpu.VMEM)
    smem = pl.BlockSpec(memory_space=pltpu.SMEM)
    hbm = pl.BlockSpec(memory_space=pltpu.HBM)
    scratch = [
        pltpu.VMEM((3, rows, half), bf),
        pltpu.VMEM((3, rows, half), bf),
        pltpu.VMEM((3, nz, slab, DH), bf),
        pltpu.VMEM((2, NY, lanes, DH), bf),
        pltpu.VMEM((2, nz, nx, slab, DH), bf),
        pltpu.VMEM((DH, nz * nx * slab), bf),
        pltpu.VMEM((2, 2, nz, lanes), f32),
        pltpu.VMEM((2, NY, DH, lanes), f32),
        pltpu.VMEM((2, NY, 8, lanes), f32),
        pltpu.VMEM((2, NY, 8, lanes), f32),
        pltpu.VMEM((2, NY, DH, lanes), bf),
        pltpu.VMEM((2, NY, 2, lanes), f32),
        pltpu.VMEM((2, NY, DH, lanes), bf),
        pltpu.VMEM((2, NY, 2, lanes), f32),
        pltpu.VMEM((2, nz // 2, 2, rows, DH), bf),
        pltpu.VMEM((2, nz, rows, DH), bf),
        pltpu.VMEM((rows, width), bf),
        pltpu.VMEM((2, nz // 4, 4, rows, DH), bf),
        pltpu.VMEM((lanes, DH), f32),
        dma((5,)),
        dma((3,)), dma((3,)),
        dma((nz,)), dma((nz,)), dma((nz,)), dma((nz,)),
        dma((2, NY)), dma((2, NY)),
        dma((nx - 1, nz // CHUNK)), dma((nx - 1, nz // CHUNK)),
        dma((2, 2, NY)), dma((2, 2, NY)), dma((2, NY)), dma((2, NY)),
        dma((2, nz)), dma((2, nz)),
        dma((7,)), dma((7,)),
    ]
    return pl.pallas_call(
        functools.partial(kernel, nz, nx),
        out_shape=jax.ShapeDtypeStruct((rows, width), bf),
        in_specs=[hbm] * 5 + [vmem] + [smem] * 3,
        out_specs=vmem,
        scratch_shapes=scratch,
        compiler_params=pltpu.CompilerParams(
            collective_id=0, has_side_effects=True, vmem_limit_bytes=63 * 2**20
        ),
        cost_estimate=pl.CostEstimate(flops=5 * 10**9, bytes_accessed=10**8, transcendentals=10**7),
        name="attend_planes",
    )(queries, keys, values, latent, entering, block_mask, levels, level_step, leaving)


def body(queries, keys, values, latent, levels, level_step, block_mask, leaving, entering):
    nz = block_mask.shape[0] // 2
    nx = lax.axis_size("head") // 4
    return updated_rows(
        nz, nx, queries, keys, values, latent, entering, block_mask, levels, level_step, leaving
    )


def solution(mesh):
    split = P(("group", "head"), None)
    placed = (split, split, split, split, P(), P(), P(), P(), P("head", "group"))
    return jax.shard_map(body, mesh=mesh, in_specs=placed, out_specs=split, check_vma=False)
```

```python
import functools

import jax
import jax.numpy as jnp
from jax import lax
from jax.experimental import pallas as pl
from jax.experimental.pallas import tpu as pltpu
from jax.sharding import PartitionSpec as P

DH = 128
MESH = pl.DeviceIdType.MESH
LOG2E = 1.4426950408889634
OFF = -1e30
EMPTY = -5e29
CHUNK = 2
WIDE = 4
PIECES = ((0, 256), (256, 128))
EARLY = 5
NY = 4


def kernel(
    nz, nx, q_ref, k_ref, v_ref, latent_ref, entering_ref, mask_ref, levels_ref, step_ref, leaving_ref, out_ref,
    mine, swap, stage, qbuf, kvbuf, vt, bias, acc, top, total,
    osend, ssend, orecv, srecv, obuf, abuf, lat, ebuf, flat,
    ls, s0s, s0r, zqs, zqr, zks, zkr, yqs, yqr, xs, xr, os_, or_, ss_, sr_, zos, zor, es, er,
):
    g = lax.axis_index("group")
    h = lax.axis_index("head")
    yh, z = lax.div(g, nz), lax.rem(g, nz)
    x, yl, core = lax.div(h, 4), lax.rem(lax.div(h, 2), 2), lax.rem(h, 2)
    y = yh * 2 + yl
    rows = latent_ref.shape[0]
    slab = 2 * rows
    half = nz * DH
    lanes = nz * slab // 2
    near = nz // 2
    keys = nx * slab
    chunks = nz // CHUNK
    scale = LOG2E / DH**0.5
    inputs = (q_ref, k_ref, v_ref)

    def dev(yy, zz, xx, cc):
        return (lax.div(yy, 2) * nz + zz, xx * 4 + lax.rem(yy, 2) * 2 + cc)

    def turn(o):
        return jnp.where(lax.rem(o, 2) == 1, lax.div(o + 1, 2), nz - lax.div(o, 2))

    def dest(o):
        return lax.rem(z + nz - turn(o), nz)

    def source(o):
        return lax.rem(z + turn(o), nz)

    def copy(src, dst, ssem, rsem, where):
        return pltpu.make_async_remote_copy(
            src_ref=src, dst_ref=dst, send_sem=ssem, recv_sem=rsem, device_id=where, device_id_type=MESH
        )

    def loop(lo, hi, f):
        def step(i, carry):
            f(i)
            return carry

        lax.fori_loop(lo, hi, step, 0)

    other = dev(y, z, x, 1 - core)
    xs_to = [lax.rem(x + d, nx) for d in (nx // 2, 1, nx - 1)]
    ys = [lax.rem(y + d, NY) for d in range(1, NY)]

    barrier = pltpu.get_barrier_semaphore()

    def greet(where):
        pl.semaphore_signal(barrier, inc=1, device_id=where, device_id_type=MESH)

    def greet_plane(o):
        greet(dev(y, dest(o), x, core))
        greet(dev(y, dest(o), x, 1 - core))

    loop(1, nz, greet_plane)
    for yy in ys:
        greet(dev(yy, z, x, core))
    for to in xs_to:
        greet(dev(y, z, to, core))
    greet(other)

    def columns(which):
        return pl.ds(pl.multiple_of(which * half, half), half)

    local = [pltpu.make_async_copy(inputs[t].at[:, columns(core)], mine.at[t], ls.at[t]) for t in range(3)]
    local.append(pltpu.make_async_copy(latent_ref, lat, ls.at[3]))
    quad, place_in_quad = lax.div(z, 4), lax.rem(z, 4)
    local.append(pltpu.make_async_copy(entering_ref, ebuf.at[yh, quad, place_in_quad], ls.at[4]))
    for c in local:
        c.start()
    pl.semaphore_wait(barrier, 1 + (nx - 1) + (NY - 1) + 2 * (nz - 1))

    def swap_copy(t):
        return copy(inputs[t].at[:, columns(1 - core)], swap.at[t], s0s.at[t], s0r.at[t], other)

    for t in range(3):
        swap_copy(t).start()

    def merge_rows(t):
        def one(zz):
            cols = pl.ds(pl.multiple_of(zz * DH, DH), DH)
            both = jnp.concatenate([mine[t, :, cols].astype(jnp.float32), swap[t, :, cols].astype(jnp.float32)], axis=0)
            stage[t, zz] = both.astype(jnp.bfloat16)

        loop(0, nz, one)

    def at_slab(zz):
        return pl.ds(pl.multiple_of(zz * slab, slab), slab)

    def place_of(o):
        return jnp.where(o < near, o, nz - 1 - o)

    def set_of(o):
        return 1 - lax.div(o, near), at_slab(place_of(o))

    def zq_copy(o):
        half_set, at = set_of(o)
        return copy(stage.at[0, dest(o)], qbuf.at[half_set, y, at], zqs.at[o], zqr.at[o], dev(y, dest(o), x, core))

    def zk_copy(o):
        return copy(stage.at[pl.ds(1, 2), dest(o)], kvbuf.at[:, o, x], zks.at[o], zkr.at[o], dev(y, dest(o), x, core))

    local[0].wait()
    swap_copy(0).wait_recv()
    merge_rows(0)
    loop(1, nz, lambda i: zq_copy(nz - i).start())
    for t in (1, 2):
        local[t].wait()
        swap_copy(t).wait_recv()
        merge_rows(t)
    loop(1, nz, lambda o: zk_copy(o).start())
    qbuf[1, y, at_slab(0)] = stage[0, z]
    kvbuf[0, 0, x] = stage[1, z]
    kvbuf[1, 0, x] = stage[2, z]

    def e_copy(n):
        if n < 3:
            block = ebuf.at[yh, quad, place_in_quad]
            where = dev(y, lax.rem(z + 4 * (n + 1), nz), x, core)
        elif n < 6:
            block = ebuf.at[yh, :, place_in_quad]
            where = dev(y, lax.rem(z + (1, 2, nz - 1)[n - 3], nz), x, core)
        else:
            block = ebuf.at[yh]
            where = dev(lax.rem(y + 2, NY), z, x, core)
        return copy(block, block, es.at[n], er.at[n], where)


    lane = lax.broadcasted_iota(jnp.int32, (2 * nz, lanes), 1)
    which = sum(jnp.where(lane >= n * slab, 1, 0) for n in range(1, near))
    row = lax.broadcasted_iota(jnp.int32, (2 * nz, lanes), 0)
    seen = mask_ref[...].astype(jnp.float32)
    for s in range(2):
        o = nz - 1 - which if s == 0 else which
        plane = z + jnp.where((o & 1) == 1, (o + 1) >> 1, nz - (o >> 1))
        plane = jnp.where(plane >= nz, plane - nz, plane)
        for b in range(2):
            pick = jnp.where(row == plane + b * nz, 1.0, 0.0).astype(jnp.float32)
            hit = lax.dot_general(seen, pick, (((0,), (0,)), ((), ())), preferred_element_type=jnp.float32)
            bias[s, b] = jnp.where(jnp.where(yh == 0, hit[:nz], hit[nz:]) > 0.5, 0.0, OFF)

    def clear(i):
        s, n = lax.div(i, NY), lax.rem(i, NY)
        acc[s, n] = jnp.zeros((DH, lanes), jnp.float32)
        top[s, n] = jnp.full((8, lanes), EMPTY, jnp.float32)
        total[s, n] = jnp.zeros((8, lanes), jnp.float32)

    loop(0, 2 * NY, clear)

    def yq_copy(s, to, frm):
        return copy(qbuf.at[s, frm], qbuf.at[s, frm], yqs.at[s, to], yqr.at[s, frm], dev(to, z, x, core))

    def share(s):
        loop(max((1 - s) * near, 1), (2 - s) * near, lambda o: zq_copy(o).wait_recv())
        for yy in ys:
            @pl.when(lax.div(yy, 2) <= yh)
            def _():
                yq_copy(s, yy, y).start()

    def shared(s):
        for yy in ys:
            @pl.when(yh <= lax.div(yy, 2))
            def _():
                yq_copy(s, y, yy).wait_recv()

    def x_copy(way, o):
        block = kvbuf.at[:, o, x]
        return copy(block, block, xs.at[way, o], xr.at[way, o], dev(y, z, xs_to[way], core))

    def bring(i):
        def one(o):
            @pl.when(o > 0)
            def _():
                zk_copy(o).wait_recv()

            for way in range(nx - 1):
                x_copy(way, o).start()

        loop(i * CHUNK, (i + 1) * CHUNK, one)

    def ready(i):
        def one(o):
            for way in range(nx - 1):
                x_copy(way, o).wait_recv()

        loop(i * CHUNK, (i + 1) * CHUNK, one)
        span = pl.ds(pl.multiple_of(i * CHUNK * keys, CHUNK * keys), CHUNK * keys)
        vt[:, span] = kvbuf[1, pl.ds(i * CHUNK, CHUNK)].reshape(CHUNK * keys, DH).T

    def attend(s, first, planes, sets):
        part = pl.ds(first, planes)
        span = pl.ds(pl.multiple_of(first * keys, CHUNK * keys), planes * keys)

        def softmax(n):
            key = kvbuf[0, part].reshape(planes * keys, DH)
            scores = lax.dot_general(
                key, qbuf[s, n], (((1,), (1,)), ((), ())), preferred_element_type=jnp.float32
            )
            old = top[s, n, 0:1]
            new = old
            pieces, shift = [], []
            for j in range(planes):
                piece = scores[j * keys : (j + 1) * keys]
                off = bias[s, n // 2, pl.ds(source(first + j), 1), :]
                pieces.append(piece)
                shift.append(off)
                new = jnp.maximum(new, jnp.max(piece, axis=0, keepdims=True) * scale + off)
            carry = jnp.exp2(old - new)
            weights = [jnp.exp2(piece * scale + (off - new)) for piece, off in zip(pieces, shift)]
            added = sum(jnp.sum(w, axis=0, keepdims=True) for w in weights)
            total[s, n, 0:1] = total[s, n, 0:1] * carry + added
            top[s, n, 0:1] = new
            return carry, jnp.concatenate([w.astype(jnp.bfloat16) for w in weights], axis=0)

        for n, (carry, rounded) in [(n, softmax(n)) for n in sets]:
            acc[s, n] = acc[s, n] * carry + jnp.dot(vt[:, span], rounded, preferred_element_type=jnp.float32)

    def o_copy(s, p, to, frm):
        part = pl.ds(*PIECES[p])
        return copy(
            osend.at[s, to, :, part], orecv.at[s, frm, :, part], os_.at[p, s, to], or_.at[p, s, frm], dev(to, z, x, core)
        )

    def s_copy(s, to, frm):
        return copy(ssend.at[s, to], srecv.at[s, frm], ss_.at[s, to], sr_.at[s, frm], dev(to, z, x, core))

    def send_part(s, n):
        @pl.when(n != y)
        def _():
            sums = total[s, n, 0:1]
            osend[s, n] = (acc[s, n] * (1.0 / jnp.maximum(sums, 1e-30))).astype(jnp.bfloat16)
            ssend[s, n, 0:1] = top[s, n, 0:1]
            ssend[s, n, 1:2] = sums
            s_copy(s, n, y).start()
            for p in range(len(PIECES)):
                o_copy(s, p, n, y).start()

    def merge(s, p):
        part = pl.ds(*PIECES[p])
        for yy in ys:
            @pl.when(lax.div(yy, 2) <= yh)
            def _():
                if p == 0:
                    s_copy(s, y, yy).wait_recv()
                o_copy(s, p, y, yy).wait_recv()
                theirs = srecv[s, yy, 0:1, part]
                old = top[s, y, 0:1, part]
                new = jnp.maximum(old, theirs)
                keep = jnp.exp2(old - new)
                gain = jnp.exp2(theirs - new) * srecv[s, yy, 1:2, part]
                acc[s, y, :, part] = acc[s, y, :, part] * keep + orecv[s, yy, :, part].astype(jnp.float32) * gain
                total[s, y, 0:1, part] = total[s, y, 0:1, part] * keep + gain
                top[s, y, 0:1, part] = new
        flat[part] = (acc[s, y, :, part] / total[s, y, 0:1, part]).T
        first, until = (0, EARLY) if p == 0 else (EARLY, near)
        some = flat[first * slab : until * slab].reshape(until - first, 2, rows, DH)
        obuf[s, first:until] = some.astype(jnp.bfloat16)

    def zo_copy(o, w):
        block = obuf.at[1 - lax.div(o, near), place_of(o), w]
        where = dev(y, source(o), x, core if w == 0 else 1 - core)
        return copy(block, abuf.at[w, o], zos.at[w, o], zor.at[w, o], where)

    def give(o):
        zo_copy(o, 0).start()
        zo_copy(o, 1).start()

    share(0)
    bring(0)
    share(1)
    bring(1)
    shared(0)

    def steps(n):
        s, w = lax.rem(n, 2), lax.div(n, 2)

        @pl.when(s == 0)
        def _():
            bring(2 * w + 2)
            ready(2 * w)
            ready(2 * w + 1)

        @pl.when(n == 1)
        def _():
            shared(1)

        @pl.when(s == 1)
        def _():
            bring(2 * w + 3)

        @pl.when(yh == 0)
        def _():
            attend(s, w * WIDE, WIDE, (2, 3, 0, 1))

        @pl.when(yh == 1)
        def _():
            attend(s, w * WIDE, WIDE, (2, 3))

    loop(0, 2 * (nz // WIDE - 1), steps)
    local[4].wait()
    for n in range(3):
        e_copy(n).start()

    def upper(n):
        s, i = lax.rem(n, 2), chunks - 2 + lax.div(n, 2)

        @pl.when(s == 0)
        def _():
            ready(i)

        attend(s, i * CHUNK, CHUNK, (2, 3))

        @pl.when(i == chunks - 1)
        def _():
            send_part(s, 2)
            send_part(s, 3)

    loop(0, 4, upper)

    def lower(s):
        attend(s, nz - WIDE, WIDE, (0, 1))
        send_part(s, 0)
        send_part(s, 1)

    @pl.when(yh == 0)
    def _():
        loop(0, 2, lower)

    for n in range(3):
        e_copy(n).wait_recv()
    for n in range(3, 6):
        e_copy(n).start()
    merge(0, 0)
    loop(0, EARLY, lambda j: give(nz - 1 - j))
    merge(0, 1)
    loop(EARLY, near, lambda j: give(nz - 1 - j))
    merge(1, 0)
    merge(1, 1)
    loop(1, near, lambda j: give(near - j))
    zo_copy(0, 1).start()
    for n in range(3, 6):
        e_copy(n).wait_recv()
    e_copy(6).start()

    leaves = leaving_ref[0] == g
    size = step_ref[levels_ref[g]]
    local[3].wait()
    e_copy(6).wait_recv()

    def update(n, block):
        cols = pl.ds(pl.multiple_of(n * DH, DH), DH)
        moved = lat[:, cols].astype(jnp.float32) + size * block.astype(jnp.float32)
        came = ebuf[lax.div(n, nz), lax.div(lax.rem(n, nz), 4), lax.rem(n, 4)].astype(jnp.float32)
        out_ref[:, cols] = jnp.where(leaves, came, moved).astype(jnp.bfloat16)

    update(core * nz + z, obuf[1, 0, 0])

    def take(o):
        zo_copy(o, 0).wait_recv()
        update(core * nz + dest(o), abuf[0, o])
        zo_copy(o, 1).wait_recv()
        update((1 - core) * nz + dest(o), abuf[1, o])

    loop(1, nz, lambda j: take(nz - j))
    zo_copy(0, 1).wait_recv()
    update((1 - core) * nz + z, abuf[1, 0])

    for t in range(3):
        swap_copy(t).wait_send()

    def sent(o):
        zq_copy(o).wait_send()
        zk_copy(o).wait_send()
        zo_copy(o, 0).wait_send()
        zo_copy(o, 1).wait_send()

    loop(1, nz, sent)
    zo_copy(0, 1).wait_send()
    for s in range(2):
        for yy in ys:
            @pl.when(lax.div(yy, 2) <= yh)
            def _():
                yq_copy(s, yy, y).wait_send()

            @pl.when(yh <= lax.div(yy, 2))
            def _():
                s_copy(s, yy, y).wait_send()
                for p in range(len(PIECES)):
                    o_copy(s, p, yy, y).wait_send()

    def x_sent(i):
        for way in range(nx - 1):
            x_copy(way, i).wait_send()

    loop(0, nz, x_sent)
    for n in range(7):
        e_copy(n).wait_send()


def updated_rows(nz, nx, queries, keys, values, latent, entering, block_mask, levels, level_step, leaving):
    rows, width = latent.shape
    slab = 2 * rows
    lanes = nz * slab // 2
    half = nz * DH
    bf, f32 = jnp.bfloat16, jnp.float32
    dma = pltpu.SemaphoreType.DMA
    vmem = pl.BlockSpec(memory_space=pltpu.VMEM)
    smem = pl.BlockSpec(memory_space=pltpu.SMEM)
    hbm = pl.BlockSpec(memory_space=pltpu.HBM)
    scratch = [
        pltpu.VMEM((3, rows, half), bf),
        pltpu.VMEM((3, rows, half), bf),
        pltpu.VMEM((3, nz, slab, DH), bf),
        pltpu.VMEM((2, NY, lanes, DH), bf),
        pltpu.VMEM((2, nz, nx, slab, DH), bf),
        pltpu.VMEM((DH, nz * nx * slab), bf),
        pltpu.VMEM((2, 2, nz, lanes), f32),
        pltpu.VMEM((2, NY, DH, lanes), f32),
        pltpu.VMEM((2, NY, 8, lanes), f32),
        pltpu.VMEM((2, NY, 8, lanes), f32),
        pltpu.VMEM((2, NY, DH, lanes), bf),
        pltpu.VMEM((2, NY, 2, lanes), f32),
        pltpu.VMEM((2, NY, DH, lanes), bf),
        pltpu.VMEM((2, NY, 2, lanes), f32),
        pltpu.VMEM((2, nz // 2, 2, rows, DH), bf),
        pltpu.VMEM((2, nz, rows, DH), bf),
        pltpu.VMEM((rows, width), bf),
        pltpu.VMEM((2, nz // 4, 4, rows, DH), bf),
        pltpu.VMEM((lanes, DH), f32),
        dma((5,)),
        dma((3,)), dma((3,)),
        dma((nz,)), dma((nz,)), dma((nz,)), dma((nz,)),
        dma((2, NY)), dma((2, NY)),
        dma((nx - 1, nz)), dma((nx - 1, nz)),
        dma((2, 2, NY)), dma((2, 2, NY)), dma((2, NY)), dma((2, NY)),
        dma((2, nz)), dma((2, nz)),
        dma((7,)), dma((7,)),
    ]
    return pl.pallas_call(
        functools.partial(kernel, nz, nx),
        out_shape=jax.ShapeDtypeStruct((rows, width), bf),
        in_specs=[hbm] * 5 + [vmem] + [smem] * 3,
        out_specs=vmem,
        scratch_shapes=scratch,
        compiler_params=pltpu.CompilerParams(
            collective_id=0, has_side_effects=True, vmem_limit_bytes=63 * 2**20
        ),
        cost_estimate=pl.CostEstimate(flops=5 * 10**9, bytes_accessed=10**8, transcendentals=10**7),
        name="attend_planes",
    )(queries, keys, values, latent, entering, block_mask, levels, level_step, leaving)


def body(queries, keys, values, latent, levels, level_step, block_mask, leaving, entering):
    nz = block_mask.shape[0] // 2
    nx = lax.axis_size("head") // 4
    return updated_rows(
        nz, nx, queries, keys, values, latent, entering, block_mask, levels, level_step, leaving
    )


def solution(mesh):
    split = P(("group", "head"), None)
    placed = (split, split, split, split, P(), P(), P(), P(), P("head", "group"))
    return jax.shard_map(body, mesh=mesh, in_specs=placed, out_specs=split, check_vma=False)
```

```python
import functools

import jax
import jax.numpy as jnp
from jax import lax
from jax.experimental import pallas as pl
from jax.experimental.pallas import tpu as pltpu
from jax.sharding import PartitionSpec as P

DH = 128
MESH = pl.DeviceIdType.MESH
LOG2E = 1.4426950408889634
OFF = -1e30
EMPTY = -5e29
CHUNK = 2
WIDE = 4
PIECES = ((0, 256), (256, 128))
EARLY = 5
NY = 4


def kernel(
    nz, nx, q_ref, k_ref, v_ref, latent_ref, entering_ref, mask_ref, levels_ref, step_ref, leaving_ref, out_ref,
    mine, swap, stage, qbuf, kvbuf, vt, bias, acc, top, total,
    osend, ssend, orecv, srecv, obuf, abuf, lat, ebuf, flat,
    ls, s0s, s0r, zqs, zqr, zks, zkr, yqs, yqr, xs, xr, os_, or_, ss_, sr_, zos, zor, es, er,
):
    g = lax.axis_index("group")
    h = lax.axis_index("head")
    yh, z = lax.div(g, nz), lax.rem(g, nz)
    x, yl, core = lax.div(h, 4), lax.rem(lax.div(h, 2), 2), lax.rem(h, 2)
    y = yh * 2 + yl
    rows = latent_ref.shape[0]
    slab = 2 * rows
    half = nz * DH
    lanes = nz * slab // 2
    near = nz // 2
    keys = nx * slab
    chunks = nz // CHUNK
    scale = LOG2E / DH**0.5
    inputs = (q_ref, k_ref, v_ref)

    def dev(yy, zz, xx, cc):
        return (lax.div(yy, 2) * nz + zz, xx * 4 + lax.rem(yy, 2) * 2 + cc)

    def turn(o):
        return jnp.where(lax.rem(o, 2) == 1, lax.div(o + 1, 2), nz - lax.div(o, 2))

    def dest(o):
        return lax.rem(z + nz - turn(o), nz)

    def source(o):
        return lax.rem(z + turn(o), nz)

    def copy(src, dst, ssem, rsem, where):
        return pltpu.make_async_remote_copy(
            src_ref=src, dst_ref=dst, send_sem=ssem, recv_sem=rsem, device_id=where, device_id_type=MESH
        )

    def loop(lo, hi, f):
        def step(i, carry):
            f(i)
            return carry

        lax.fori_loop(lo, hi, step, 0)

    other = dev(y, z, x, 1 - core)
    xs_to = [lax.rem(x + d, nx) for d in (nx // 2, 1, nx - 1)]
    ys = [lax.rem(y + d, NY) for d in range(1, NY)]

    barrier = pltpu.get_barrier_semaphore()

    def greet(where):
        pl.semaphore_signal(barrier, inc=1, device_id=where, device_id_type=MESH)

    def greet_plane(o):
        greet(dev(y, dest(o), x, core))
        greet(dev(y, dest(o), x, 1 - core))

    loop(1, nz, greet_plane)
    for yy in ys:
        greet(dev(yy, z, x, core))
    for to in xs_to:
        greet(dev(y, z, to, core))
    greet(other)

    def columns(which):
        return pl.ds(pl.multiple_of(which * half, half), half)

    local = [pltpu.make_async_copy(inputs[t].at[:, columns(core)], mine.at[t], ls.at[t]) for t in range(3)]
    local.append(pltpu.make_async_copy(latent_ref, lat, ls.at[3]))
    quad, place_in_quad = lax.div(z, 4), lax.rem(z, 4)
    local.append(pltpu.make_async_copy(entering_ref, ebuf.at[yh, quad, place_in_quad], ls.at[4]))
    for c in local:
        c.start()
    pl.semaphore_wait(barrier, 1 + (nx - 1) + (NY - 1) + 2 * (nz - 1))

    def swap_copy(t):
        return copy(inputs[t].at[:, columns(1 - core)], swap.at[t], s0s.at[t], s0r.at[t], other)

    for t in range(3):
        swap_copy(t).start()

    def merge_rows(t):
        def one(zz):
            cols = pl.ds(pl.multiple_of(zz * DH, DH), DH)
            both = jnp.concatenate([mine[t, :, cols].astype(jnp.float32), swap[t, :, cols].astype(jnp.float32)], axis=0)
            stage[t, zz] = both.astype(jnp.bfloat16)

        loop(0, nz, one)

    def at_slab(zz):
        return pl.ds(pl.multiple_of(zz * slab, slab), slab)

    def place_of(o):
        return jnp.where(o < near, o, nz - 1 - o)

    def set_of(o):
        return 1 - lax.div(o, near), at_slab(place_of(o))

    def zq_copy(o):
        half_set, at = set_of(o)
        return copy(stage.at[0, dest(o)], qbuf.at[half_set, y, at], zqs.at[o], zqr.at[o], dev(y, dest(o), x, core))

    def zk_copy(o):
        return copy(stage.at[pl.ds(1, 2), dest(o)], kvbuf.at[:, o, x], zks.at[o], zkr.at[o], dev(y, dest(o), x, core))

    local[0].wait()
    swap_copy(0).wait_recv()
    merge_rows(0)
    loop(1, nz, lambda i: zq_copy(nz - i).start())
    for t in (1, 2):
        local[t].wait()
        swap_copy(t).wait_recv()
        merge_rows(t)
    loop(1, nz, lambda o: zk_copy(o).start())
    qbuf[1, y, at_slab(0)] = stage[0, z]
    kvbuf[0, 0, x] = stage[1, z]
    kvbuf[1, 0, x] = stage[2, z]

    def e_copy(n):
        if n < 3:
            block = ebuf.at[yh, quad, place_in_quad]
            where = dev(y, lax.rem(z + 4 * (n + 1), nz), x, core)
        elif n < 6:
            block = ebuf.at[yh, :, place_in_quad]
            where = dev(y, lax.rem(z + (1, 2, nz - 1)[n - 3], nz), x, core)
        else:
            block = ebuf.at[yh]
            where = dev(lax.rem(y + 2, NY), z, x, core)
        return copy(block, block, es.at[n], er.at[n], where)


    lane = lax.broadcasted_iota(jnp.int32, (2 * nz, lanes), 1)
    which = sum(jnp.where(lane >= n * slab, 1, 0) for n in range(1, near))
    row = lax.broadcasted_iota(jnp.int32, (2 * nz, lanes), 0)
    seen = mask_ref[...].astype(jnp.float32)
    for s in range(2):
        o = nz - 1 - which if s == 0 else which
        plane = z + jnp.where((o & 1) == 1, (o + 1) >> 1, nz - (o >> 1))
        plane = jnp.where(plane >= nz, plane - nz, plane)
        for b in range(2):
            pick = jnp.where(row == plane + b * nz, 1.0, 0.0).astype(jnp.float32)
            hit = lax.dot_general(seen, pick, (((0,), (0,)), ((), ())), preferred_element_type=jnp.float32)
            bias[s, b] = jnp.where(jnp.where(yh == 0, hit[:nz], hit[nz:]) > 0.5, 0.0, OFF)

    def clear(i):
        s, n = lax.div(i, NY), lax.rem(i, NY)
        acc[s, n] = jnp.zeros((DH, lanes), jnp.float32)
        top[s, n] = jnp.full((8, lanes), EMPTY, jnp.float32)
        total[s, n] = jnp.zeros((8, lanes), jnp.float32)

    loop(0, 2 * NY, clear)

    def yq_copy(s, to, frm):
        return copy(qbuf.at[s, frm], qbuf.at[s, frm], yqs.at[s, to], yqr.at[s, frm], dev(to, z, x, core))

    def share(s):
        loop(max((1 - s) * near, 1), (2 - s) * near, lambda o: zq_copy(o).wait_recv())
        for yy in ys:
            @pl.when(lax.div(yy, 2) <= yh)
            def _():
                yq_copy(s, yy, y).start()

    def shared(s):
        for yy in ys:
            @pl.when(yh <= lax.div(yy, 2))
            def _():
                yq_copy(s, y, yy).wait_recv()

    def x_copy(way, i):
        block = kvbuf.at[:, pl.ds(i * CHUNK, CHUNK), x]
        return copy(block, block, xs.at[way, i], xr.at[way, i], dev(y, z, xs_to[way], core))

    def bring(i):
        first = 1 if isinstance(i, int) and i == 0 else i * CHUNK
        loop(first, (i + 1) * CHUNK, lambda o: zk_copy(o).wait_recv())
        for way in range(nx - 1):
            x_copy(way, i).start()

    def ready(i):
        for way in range(nx - 1):
            x_copy(way, i).wait_recv()
        span = pl.ds(pl.multiple_of(i * CHUNK * keys, CHUNK * keys), CHUNK * keys)
        vt[:, span] = kvbuf[1, pl.ds(i * CHUNK, CHUNK)].reshape(CHUNK * keys, DH).T

    def attend(s, first, planes, sets):
        part = pl.ds(first, planes)
        span = pl.ds(pl.multiple_of(first * keys, CHUNK * keys), planes * keys)

        def softmax(n):
            key = kvbuf[0, part].reshape(planes * keys, DH)
            scores = lax.dot_general(
                key, qbuf[s, n], (((1,), (1,)), ((), ())), preferred_element_type=jnp.float32
            )
            old = top[s, n, 0:1]
            new = old
            pieces, shift = [], []
            for j in range(planes):
                piece = scores[j * keys : (j + 1) * keys]
                off = bias[s, n // 2, pl.ds(source(first + j), 1), :]
                pieces.append(piece)
                shift.append(off)
                new = jnp.maximum(new, jnp.max(piece, axis=0, keepdims=True) * scale + off)
            carry = jnp.exp2(old - new)
            weights = [jnp.exp2(piece * scale + (off - new)) for piece, off in zip(pieces, shift)]
            added = sum(jnp.sum(w, axis=0, keepdims=True) for w in weights)
            total[s, n, 0:1] = total[s, n, 0:1] * carry + added
            top[s, n, 0:1] = new
            return carry, jnp.concatenate([w.astype(jnp.bfloat16) for w in weights], axis=0)

        for n, (carry, rounded) in [(n, softmax(n)) for n in sets]:
            acc[s, n] = acc[s, n] * carry + jnp.dot(vt[:, span], rounded, preferred_element_type=jnp.float32)

    def o_copy(s, p, to, frm):
        part = pl.ds(*PIECES[p])
        return copy(
            osend.at[s, to, :, part], orecv.at[s, frm, :, part], os_.at[p, s, to], or_.at[p, s, frm], dev(to, z, x, core)
        )

    def s_copy(s, to, frm):
        return copy(ssend.at[s, to], srecv.at[s, frm], ss_.at[s, to], sr_.at[s, frm], dev(to, z, x, core))

    def send_part(s, n):
        @pl.when(n != y)
        def _():
            sums = total[s, n, 0:1]
            osend[s, n] = (acc[s, n] * (1.0 / jnp.maximum(sums, 1e-30))).astype(jnp.bfloat16)
            ssend[s, n, 0:1] = top[s, n, 0:1]
            ssend[s, n, 1:2] = sums
            s_copy(s, n, y).start()
            for p in range(len(PIECES)):
                o_copy(s, p, n, y).start()

    def merge(s, p):
        part = pl.ds(*PIECES[p])
        for yy in ys:
            @pl.when(lax.div(yy, 2) <= yh)
            def _():
                if p == 0:
                    s_copy(s, y, yy).wait_recv()
                o_copy(s, p, y, yy).wait_recv()
                theirs = srecv[s, yy, 0:1, part]
                old = top[s, y, 0:1, part]
                new = jnp.maximum(old, theirs)
                keep = jnp.exp2(old - new)
                gain = jnp.exp2(theirs - new) * srecv[s, yy, 1:2, part]
                acc[s, y, :, part] = acc[s, y, :, part] * keep + orecv[s, yy, :, part].astype(jnp.float32) * gain
                total[s, y, 0:1, part] = total[s, y, 0:1, part] * keep + gain
                top[s, y, 0:1, part] = new
        flat[part] = (acc[s, y, :, part] / total[s, y, 0:1, part]).T
        first, until = (0, EARLY) if p == 0 else (EARLY, near)
        some = flat[first * slab : until * slab].reshape(until - first, 2, rows, DH)
        obuf[s, first:until] = some.astype(jnp.bfloat16)

    def zo_copy(o, w):
        block = obuf.at[1 - lax.div(o, near), place_of(o), w]
        where = dev(y, source(o), x, core if w == 0 else 1 - core)
        return copy(block, abuf.at[w, o], zos.at[w, o], zor.at[w, o], where)

    def give(o):
        zo_copy(o, 0).start()
        zo_copy(o, 1).start()

    share(0)
    bring(0)
    share(1)
    bring(1)
    shared(0)

    def steps(n):
        s, w = lax.rem(n, 2), lax.div(n, 2)

        @pl.when(s == 0)
        def _():
            bring(2 * w + 2)
            ready(2 * w)
            ready(2 * w + 1)

        @pl.when(n == 1)
        def _():
            shared(1)

        @pl.when(s == 1)
        def _():
            bring(2 * w + 3)

        @pl.when(yh == 0)
        def _():
            attend(s, w * WIDE, WIDE, (2, 3, 0, 1))

        @pl.when(yh == 1)
        def _():
            attend(s, w * WIDE, WIDE, (2, 3))

    loop(0, 2 * (nz // WIDE - 1), steps)
    local[4].wait()
    for n in range(3):
        e_copy(n).start()

    def upper(n):
        s, i = lax.rem(n, 2), chunks - 2 + lax.div(n, 2)

        @pl.when(s == 0)
        def _():
            ready(i)

        attend(s, i * CHUNK, CHUNK, (2, 3))

        @pl.when(i == chunks - 1)
        def _():
            send_part(s, 2)
            send_part(s, 3)

    loop(0, 4, upper)

    def lower(s):
        attend(s, nz - WIDE, WIDE, (0, 1))
        send_part(s, 0)
        send_part(s, 1)

    @pl.when(yh == 0)
    def _():
        loop(0, 2, lower)

    for n in range(3):
        e_copy(n).wait_recv()
    for n in range(3, 6):
        e_copy(n).start()

    for t in range(3):
        swap_copy(t).wait_send()

    def left(o):
        zq_copy(o).wait_send()
        zk_copy(o).wait_send()

    loop(1, nz, left)
    for s in range(2):
        for yy in ys:
            @pl.when(lax.div(yy, 2) <= yh)
            def _():
                yq_copy(s, yy, y).wait_send()

    def x_sent(i):
        for way in range(nx - 1):
            x_copy(way, i).wait_send()

    loop(0, chunks, x_sent)

    merge(0, 0)
    loop(0, EARLY, lambda j: give(nz - 1 - j))
    merge(0, 1)
    loop(EARLY, near, lambda j: give(nz - 1 - j))
    merge(1, 0)
    merge(1, 1)
    loop(1, near, lambda j: give(near - j))
    zo_copy(0, 1).start()
    for n in range(3, 6):
        e_copy(n).wait_recv()
    e_copy(6).start()

    leaves = leaving_ref[0] == g
    size = step_ref[levels_ref[g]]
    local[3].wait()
    e_copy(6).wait_recv()

    def update(n, block):
        cols = pl.ds(pl.multiple_of(n * DH, DH), DH)
        moved = lat[:, cols].astype(jnp.float32) + size * block.astype(jnp.float32)
        came = ebuf[lax.div(n, nz), lax.div(lax.rem(n, nz), 4), lax.rem(n, 4)].astype(jnp.float32)
        out_ref[:, cols] = jnp.where(leaves, came, moved).astype(jnp.bfloat16)

    update(core * nz + z, obuf[1, 0, 0])

    def take(o):
        zo_copy(o, 0).wait_recv()
        update(core * nz + dest(o), abuf[0, o])
        zo_copy(o, 1).wait_recv()
        update((1 - core) * nz + dest(o), abuf[1, o])

    loop(1, nz, lambda j: take(nz - j))
    zo_copy(0, 1).wait_recv()
    update((1 - core) * nz + z, abuf[1, 0])

    def sent(o):
        zo_copy(o, 0).wait_send()
        zo_copy(o, 1).wait_send()

    loop(1, nz, sent)
    zo_copy(0, 1).wait_send()
    for s in range(2):
        for yy in ys:
            @pl.when(yh <= lax.div(yy, 2))
            def _():
                s_copy(s, yy, y).wait_send()
                for p in range(len(PIECES)):
                    o_copy(s, p, yy, y).wait_send()

    for n in range(7):
        e_copy(n).wait_send()


def updated_rows(nz, nx, queries, keys, values, latent, entering, block_mask, levels, level_step, leaving):
    rows, width = latent.shape
    slab = 2 * rows
    lanes = nz * slab // 2
    half = nz * DH
    bf, f32 = jnp.bfloat16, jnp.float32
    dma = pltpu.SemaphoreType.DMA
    vmem = pl.BlockSpec(memory_space=pltpu.VMEM)
    smem = pl.BlockSpec(memory_space=pltpu.SMEM)
    hbm = pl.BlockSpec(memory_space=pltpu.HBM)
    scratch = [
        pltpu.VMEM((3, rows, half), bf),
        pltpu.VMEM((3, rows, half), bf),
        pltpu.VMEM((3, nz, slab, DH), bf),
        pltpu.VMEM((2, NY, lanes, DH), bf),
        pltpu.VMEM((2, nz, nx, slab, DH), bf),
        pltpu.VMEM((DH, nz * nx * slab), bf),
        pltpu.VMEM((2, 2, nz, lanes), f32),
        pltpu.VMEM((2, NY, DH, lanes), f32),
        pltpu.VMEM((2, NY, 8, lanes), f32),
        pltpu.VMEM((2, NY, 8, lanes), f32),
        pltpu.VMEM((2, NY, DH, lanes), bf),
        pltpu.VMEM((2, NY, 2, lanes), f32),
        pltpu.VMEM((2, NY, DH, lanes), bf),
        pltpu.VMEM((2, NY, 2, lanes), f32),
        pltpu.VMEM((2, nz // 2, 2, rows, DH), bf),
        pltpu.VMEM((2, nz, rows, DH), bf),
        pltpu.VMEM((rows, width), bf),
        pltpu.VMEM((2, nz // 4, 4, rows, DH), bf),
        pltpu.VMEM((lanes, DH), f32),
        dma((5,)),
        dma((3,)), dma((3,)),
        dma((nz,)), dma((nz,)), dma((nz,)), dma((nz,)),
        dma((2, NY)), dma((2, NY)),
        dma((nx - 1, nz // CHUNK)), dma((nx - 1, nz // CHUNK)),
        dma((2, 2, NY)), dma((2, 2, NY)), dma((2, NY)), dma((2, NY)),
        dma((2, nz)), dma((2, nz)),
        dma((7,)), dma((7,)),
    ]
    return pl.pallas_call(
        functools.partial(kernel, nz, nx),
        out_shape=jax.ShapeDtypeStruct((rows, width), bf),
        in_specs=[hbm] * 5 + [vmem] + [smem] * 3,
        out_specs=vmem,
        scratch_shapes=scratch,
        compiler_params=pltpu.CompilerParams(
            collective_id=0, has_side_effects=True, vmem_limit_bytes=63 * 2**20
        ),
        cost_estimate=pl.CostEstimate(flops=5 * 10**9, bytes_accessed=10**8, transcendentals=10**7),
        name="attend_planes",
    )(queries, keys, values, latent, entering, block_mask, levels, level_step, leaving)


def body(queries, keys, values, latent, levels, level_step, block_mask, leaving, entering):
    nz = block_mask.shape[0] // 2
    nx = lax.axis_size("head") // 4
    return updated_rows(
        nz, nx, queries, keys, values, latent, entering, block_mask, levels, level_step, leaving
    )


def solution(mesh):
    split = P(("group", "head"), None)
    placed = (split, split, split, split, P(), P(), P(), P(), P("head", "group"))
    return jax.shard_map(body, mesh=mesh, in_specs=placed, out_specs=split, check_vma=False)
```
